32 devices in a mesh: lat: 8 (over z, x), lon: 4 (over y, core).
Axes of the slice: x: 2, y: 2, z: 4, core: 2. Of those that a mesh axis runs over, the one named last changes fastest.
Arguments:
- spectra: bfloat16 [32768, 8448], P(('lat', 'lon')), may hold values from -6 to 6
- pc_basis: bfloat16 [8448, 256], replicated, may hold values from -0.0625 to 0.0625
- destination: int32 [32768, 1], P(('lat', 'lon')), may hold values from 0 to 31; in each aligned block of 1024 rows (0 to 1023, 1024 to 2047, ...) at most 64 rows name the same one
- corner_row: int32 [32768], P(('lat', 'lon')), may hold values from 0 to 64
- corner_col: int32 [32768], P(('lat', 'lon')), may hold values from 0 to 64
- corner_weight: bfloat16 [32768, 4], P(('lat', 'lon')), may hold values from 0 to 1
- state: bfloat16 [512, 256, 128], P('lat', 'lon'), may hold values from -6 to 6
- inv_sigma: float32 [256], replicated, may hold values from 0.5 to 2
- w_in: bfloat16 [128, 512], replicated, may hold values from -0.5 to 0.5
- b_in: float32 [512], replicated, may hold values from -3 to 3
- w_out: bfloat16 [512, 256], replicated, may hold values from -0.25 to 0.25
- b_out: float32 [256], replicated, may hold values from -3 to 3
Outputs:
- departures: bfloat16 [32768, 256], P(('lat', 'lon'))
- state_gradient: float32 [512, 256, 128], P('lat', 'lon')
The draws below stay inside these ranges and needn't reach their ends.
Inputs may be any that keep to these rules, and one draw needn't show every extreme that they name: `destination`: in the rows of one device no tile is named by more than 64 spectra, a bound that some block reaches.
All inputs are finite; a program needn't handle non-finite values.
Results may differ from the reference program's by a relative error of at most 0.0075.
Values may be sent and summed in bfloat16 or wider, within the bound.
A program may use at most 128 MiB of HBM per device.

```python
import math
import jax
import jax.numpy as jnp
import numpy as np
from jax import lax

NCH = 8448
NPC = 256
LEV = 128
HID = 512
OBS_DEV = 1024
ROWS_T = 64
COLS_T = 64
CAP = 64
OBS = 32768
NLAT = 512
NLON = 256
N_LAT = 8
N_LON = 4


def touch_ends(result, rng, low, largest):
    index_at = [jax.random.randint(jax.random.fold_in(rng, axis), (), 0, length) for axis, length in enumerate(result.shape)]
    widest = result.shape.index(max(result.shape))
    next_to = index_at[:widest] + [(index_at[widest] + 1) % result.shape[widest]] + index_at[widest + 1:]
    return result.at[tuple(index_at)].set(low).at[tuple(next_to)].set(largest)


def level_of(rng, shape, split, smallest, largest):
    loudness = 1.0
    for axis_at, shards_of in split:
        heights = jax.random.uniform(jax.random.fold_in(jax.random.fold_in(rng, 6), axis_at), (shards_of,), jnp.float32, smallest / len(split), largest / len(split))
        loudness = loudness * jnp.repeat(jnp.exp(heights), shape[axis_at] // shards_of).reshape((-1,) + (1,) * (len(shape) - 1 - axis_at))
    return loudness


def routed_block(stream_key, own, number, rows, count, top, reach, lean):
    sequence = jax.random.permutation(stream_key, count)
    packed, ordinary = load_shares(count, rows * top, reach, lean, True), load_shares(count, rows * top, reach, lean, False)
    places = jnp.arange(count)

    def named(sizes, offset_by):
        used = int((sizes > 0).sum())
        fixed = max(1, used // 4)
        passed = fixed + (places - fixed + offset_by * (used - fixed)) % max(1, count - fixed)
        return jnp.zeros((count,), jnp.int32).at[sequence[jnp.where(places < fixed, places, passed)]].set(jnp.asarray(sizes, jnp.int32))

    sizes = jnp.where(number % 4 == 0, named(packed, number // 4), named(ordinary, number - number // 4 - 1))
    mixed = jax.random.permutation(jax.random.fold_in(own, 3), count)
    donor, taker = mixed[0:count // 2 * 2:2], mixed[1:count // 2 * 2:2]
    margin = jnp.minimum(sizes[donor] - 1, reach - sizes[taker]) // 2
    margin = jnp.where((donor == sequence[0]) | (taker == sequence[0]) | (sizes[taker] == 0), 0, jnp.maximum(margin, 0))
    passed = jax.random.randint(jax.random.fold_in(own, 4), (count // 2,), 0, 1 << 20) % (margin + 1)
    sizes = sizes.at[donor].add(-passed).at[taker].add(passed)
    items = jnp.searchsorted(jnp.cumsum(sizes), jnp.arange(rows * top), side="right").astype(jnp.int32)
    table = items.reshape(top, rows).T
    table = table[jax.random.permutation(jax.random.fold_in(own, 1), rows)]
    offset_by = jax.random.randint(jax.random.fold_in(own, 2), (rows, 1), 0, top)
    return jnp.take_along_axis(table, (jnp.arange(top)[None, :] + offset_by) % top, axis=1)


def load_shares(number_of, total, most, skew, full):
    loads = [(1 << 20) // math.isqrt(rank ** skew) + 1 for rank in range(1, number_of + 1)]
    largest = most if full else min(most, max(-(-total // number_of), total * loads[0] // sum(loads)))
    least = 1 if total - largest >= number_of - 1 else 0
    holding, rest = [largest] + [least] * (number_of - 1), total - largest - least * (number_of - 1)
    while rest > 0:
        candidates = [i for i in range(1, number_of) if holding[i] < largest] or [i for i in range(1, number_of) if holding[i] < most]
        pool, remaining = sum([loads[i] for i in candidates]), rest
        for i in candidates:
            more = min(most - holding[i], max(1, remaining * loads[i] // pool), rest)
            holding[i] = holding[i] + more
            rest = rest - more
    return np.array(holding)


def scatter_about(key, shape, width, reach, cuts=(), dtype=jnp.bfloat16):
    result = jax.random.normal(key, shape, jnp.float32) * width
    if len(cuts) > 0:
        result = level_of(key, shape, cuts, -0.22, 0.18) * result
    return jnp.clip(result, min=-reach, max=reach).astype(dtype)


def setup_inputs(seed: int = 0) -> dict:
    key_of = jax.random.split(jax.random.key(seed), 13)
    spectra = scatter_about(key_of[0], (OBS, NCH), 1.0, 6.0, ((0, 32),))
    pc_basis = scatter_about(key_of[1], (NCH, NPC), NCH ** -0.5, 0.0625)
    destination_keys = jax.random.split(jax.random.fold_in(key_of[2], 1), OBS // OBS_DEV)
    destination_turns = jax.random.permutation(jax.random.fold_in(key_of[2], 3), OBS // OBS_DEV)
    destination = jax.vmap(lambda own, number: routed_block(jax.random.fold_in(key_of[2], 2), own, number, OBS_DEV, N_LAT * N_LON, 1, CAP, 2))(destination_keys, destination_turns).reshape((OBS, 1))
    corner_row = touch_ends(jax.random.randint(key_of[3], (OBS,), 0, ROWS_T + 1), jax.random.fold_in(key_of[3], 1), 0, ROWS_T).astype(jnp.int32)
    corner_col = touch_ends(jax.random.randint(key_of[4], (OBS,), 0, COLS_T + 1), jax.random.fold_in(key_of[4], 1), 0, COLS_T).astype(jnp.int32)
    corner_weight = jnp.clip(1.0 * jax.random.uniform(key_of[5], (OBS, 4), jnp.float32) ** level_of(key_of[5], (OBS, 4), ((0, 32),), -0.2, 0.2), 0.0, 1.0).astype(jnp.bfloat16)
    state = scatter_about(key_of[6], (NLAT, NLON, LEV), 1.0, 6.0, ((0, 8), (1, 4)))
    inv_sigma = jnp.clip(jnp.exp(jax.random.uniform(key_of[7], (NPC,), jnp.float32, math.log(0.5), math.log(2.0))), 0.5, 2.0)
    w_in = scatter_about(key_of[8], (LEV, HID), LEV ** -0.5, 0.5)
    b_in = scatter_about(key_of[9], (HID,), 0.5, 3.0, (), jnp.float32)
    w_out = scatter_about(key_of[10], (HID, NPC), HID ** -0.5, 0.25)
    b_out = scatter_about(key_of[11], (NPC,), 0.5, 3.0, (), jnp.float32)
    return {"spectra": spectra, "pc_basis": pc_basis, "destination": destination, "corner_row": corner_row, "corner_col": corner_col, "corner_weight": corner_weight, "state": state, "inv_sigma": inv_sigma, "w_in": w_in, "b_in": b_in, "w_out": w_out, "b_out": b_out}


def reference(spectra, pc_basis, destination, corner_row, corner_col, corner_weight, state, inv_sigma, w_in, b_in, w_out, b_out):
    blocks = spectra.reshape(N_LAT * N_LON, OBS_DEV, NCH)
    pcs = lax.map(lambda block: jnp.dot(block, pc_basis, preferred_element_type=jnp.float32).astype(jnp.bfloat16), blocks)
    pcs = pcs.reshape(-1, NPC)
    dest = destination[:, 0]
    band = dest // N_LON
    quarter = dest % N_LON
    nlon = COLS_T * N_LON
    padded = jnp.pad(state, ((1, 1), (0, 0), (0, 0)))
    rows_base = band * ROWS_T + corner_row
    cols_base = quarter * COLS_T + corner_col - 1
    offsets = [(0, 0), (1, 0), (0, 1), (1, 1)]
    weights = corner_weight.astype(jnp.float32)
    column = jnp.zeros((dest.shape[0], LEV), jnp.float32)
    places = []
    for k in range(4):
        rows_k = (rows_base + offsets[k][0]).astype(jnp.int32)
        cols_k = ((cols_base + offsets[k][1]) % nlon).astype(jnp.int32)
        places.append((rows_k, cols_k))
        column = column + weights[:, k:k + 1] * padded[rows_k, cols_k].astype(jnp.float32)
    column = column.astype(jnp.bfloat16)
    pre = jnp.dot(column, w_in, preferred_element_type=jnp.float32) + b_in
    hidden = jax.nn.silu(pre).astype(jnp.bfloat16)
    sim = jnp.dot(hidden, w_out, preferred_element_type=jnp.float32) + b_out
    dep = (sim - pcs.astype(jnp.float32)) * inv_sigma
    g_sim = (dep * inv_sigma).astype(jnp.bfloat16)
    g_hidden = jnp.dot(g_sim, w_out.T, preferred_element_type=jnp.float32)
    sig = jax.nn.sigmoid(pre)
    g_pre = (g_hidden * sig * (1.0 + pre * (1.0 - sig))).astype(jnp.bfloat16)
    g_column = jnp.dot(g_pre, w_in.T, preferred_element_type=jnp.float32)
    grad = jnp.zeros(padded.shape, jnp.float32)
    for k in range(4):
        grad = grad.at[places[k][0], places[k][1]].add(weights[:, k:k + 1] * g_column)
    return dep.astype(jnp.bfloat16), grad[1:-1]
```

```python
import functools

import jax
import jax.numpy as jnp
from jax import lax
from jax.experimental import pallas as pl
from jax.experimental.pallas import tpu as pltpu
from jax.sharding import PartitionSpec as P

MESH = pl.DeviceIdType.MESH
BF = jnp.bfloat16
F32 = jnp.float32
LANES = 128


def dot(a, b, dims=((1,), (0,))):
    return lax.dot_general(a, b, (dims, ((), ())), preferred_element_type=F32)


def rim_table(R, C):
    own = R * C
    ns, west, east = own, own + LANES, own + 2 * LANES
    tall = R + 16
    return [
        (-1, 0, 0, ns, C),
        (1, 0, (R - 1) * C, ns + C, C),
        (0, -1, None, east, tall),
        (0, 1, None, west + 16, tall),
        (-1, -1, 0, east + 112, 16),
        (-1, 1, C - 16, west + 112, 16),
        (1, -1, (R - 1) * C, east + 96, 16),
        (1, 1, own - 16, west + 96, 16),
    ]


def kernel(
    n_lat, n_lon, cap, R, C,
    meta_ref, state_hbm, spectra_hbm, basis_hbm, w_in_ref, b_in_ref, w_out_ref, b_out_ref, inv_ref,
    dep_hbm, grad_hbm,
    spectra_v, basis_v, pcs_v, onehot, send_meta, recv_meta, rows_v, f_sl, q_sl, f_ls, q_ls,
    cells, edges, column, pulled, g_send, g_recv, dep_slot, dep_v, total, rim_in,
    in_sem, state_sem, out_sem,
    meta_send, meta_recv, halo_send, halo_recv, col_send, col_recv, grad_send, grad_recv,
    rim_send, rim_recv,
):
    n = n_lat * n_lon
    lat = lax.axis_index("lat")
    lon = lax.axis_index("lon")
    me = lat * n_lon + lon
    slots = n * cap
    G = 256
    per = G // cap
    groups = slots // G
    mine = me // per
    own = R * C
    chunks = cells.shape[0] // LANES
    obs = meta_ref.shape[1]
    parts = obs // G
    table = rim_table(R, C)

    def at(peer):
        return (peer // n_lon, lax.rem(peer, n_lon))

    def near(dl, dc):
        return (lax.rem(lat + dl + n_lat, n_lat), lax.rem(lon + dc + n_lon, n_lon))

    barrier = pltpu.get_barrier_semaphore()

    def greet(j, carry):
        peer = lax.rem(me + j, n)
        pl.semaphore_signal(barrier, inc=1, device_id=at(peer), device_id_type=MESH)
        return carry

    lax.fori_loop(1, n, greet, 0)

    state_copy = pltpu.make_async_copy(state_hbm, cells.at[pl.ds(0, own)], state_sem)
    state_copy.start()
    basis_copy = pltpu.make_async_copy(basis_hbm, basis_v, in_sem.at[parts])
    basis_copy.start()

    def spectra_copy(i):
        rows = pl.ds(i * G, G)
        return pltpu.make_async_copy(spectra_hbm.at[rows], spectra_v.at[rows], in_sem.at[i])

    for i in range(parts):
        spectra_copy(i).start()

    dest = meta_ref[6:7, :]
    before = lax.broadcasted_iota(jnp.int32, (LANES, LANES), 0)
    after = lax.broadcasted_iota(jnp.int32, (LANES, LANES), 1)
    upto = jnp.where(before <= after, 1.0, 0.0).astype(BF)
    tile_id = lax.broadcasted_iota(jnp.int32, (n, LANES), 0).astype(F32)
    carry = jnp.zeros((n, 1), F32)
    places = []
    for b in range(obs // LANES):
        d = dest[:, b * LANES : (b + 1) * LANES]
        oh = jnp.where(tile_id == d, 1.0, 0.0)
        rank = dot(oh.astype(BF), upto) + carry
        slot = jnp.sum(rank * oh, axis=0, keepdims=True) - 1.0
        places.append(d * cap + slot)
        carry = carry + jnp.sum(oh, axis=1, keepdims=True)
    place = jnp.concatenate(places, axis=1)
    meta = meta_ref[...].astype(BF)

    def pack(g, carry):
        ids = (lax.broadcasted_iota(jnp.int32, (G, obs), 0) + g * G).astype(F32)
        sel = jnp.where(ids == place, 1.0, 0.0).astype(BF)
        onehot[pl.ds(g * G, G), :] = sel
        res = dot(meta, sel, ((1,), (1,)))
        for i in range(per):
            piece = res[:, i * cap : (i + 1) * cap]
            send_meta[g * per + i] = jnp.concatenate(
                [piece, jnp.zeros((8, LANES - cap), F32)], axis=1
            )
        return carry

    lax.fori_loop(0, groups, pack, 0)

    pl.semaphore_wait(barrier, n - 1)

    def push_meta(j, carry):
        peer = lax.rem(me + j, n)
        pltpu.make_async_remote_copy(
            src_ref=send_meta.at[peer],
            dst_ref=recv_meta.at[me],
            send_sem=meta_send,
            recv_sem=meta_recv,
            device_id=at(peer),
            device_id_type=MESH,
        ).start()
        return carry

    lax.fori_loop(1, n, push_meta, 0)
    self_meta = pltpu.make_async_copy(send_meta.at[me], recv_meta.at[me], meta_recv)
    self_meta.start()

    west0 = own + LANES
    cells[pl.ds(west0, 16), :] = jnp.zeros((16, LANES), BF)
    cells[pl.ds(west0 + LANES + 80, 16), :] = jnp.zeros((16, LANES), BF)
    state_copy.wait()
    tall = R + 16
    row = lax.broadcasted_iota(jnp.int32, (tall, own), 0)
    cell = lax.broadcasted_iota(jnp.int32, (tall, own), 1)
    cut = R - 16
    row = jnp.where(row < cut, row, jnp.where(row < R, -R, row - 16))
    for s, c in ((0, 0), (1, C - 1)):
        pick = jnp.where(cell == row * C + c, 1.0, 0.0).astype(BF)
        edges[s] = dot(pick, cells[pl.ds(0, own), :]).astype(BF)

    def halo(k):
        dl, dc, src, dst, rows = table[k]
        if src is None:
            source = edges.at[0 if dc < 0 else 1]
        else:
            source = cells.at[pl.ds(src, rows)]
        return pltpu.make_async_remote_copy(
            src_ref=source,
            dst_ref=cells.at[pl.ds(dst, rows)],
            send_sem=halo_send.at[k],
            recv_sem=halo_recv.at[k],
            device_id=near(dl, dc),
            device_id_type=MESH,
        )

    for k in range(8):
        halo(k).start()

    def components(i, carry):
        spectra_copy(i).wait()
        rows = pl.ds(i * G, G)
        pcs_v[rows, :] = dot(spectra_v[rows, :], basis_v[...]).astype(BF)
        return carry

    basis_copy.wait()
    half = parts // 2
    lax.fori_loop(0, half, components, 0)

    pltpu.make_async_copy(recv_meta, recv_meta, meta_recv).wait()
    for s in range(n):
        rows_v[:, s * cap : (s + 1) * cap] = recv_meta[s][:, 0:cap]

    def spread(g, carry):
        rows = pl.ds(pl.multiple_of(g * G, G), G)
        m = rows_v[:, rows]
        r0 = m[4:5].astype(jnp.int32) - 1
        c0 = m[5:6].astype(jnp.int32) - 1
        level = lax.broadcasted_iota(jnp.int32, (LANES, G), 0)
        f = jnp.zeros((LANES, G), F32)
        q = jnp.full((LANES, G), -1.0, F32)
        for k, (dr, dc) in enumerate(((0, 0), (1, 0), (0, 1), (1, 1))):
            r, c = r0 + dr, c0 + dc
            north, south = r < 0, r >= R
            on_w, on_e = c < 0, c >= C
            chunk = jnp.where(
                on_w, chunks - 2,
                jnp.where(on_e, chunks - 1, jnp.where(north | south, chunks - 3, r >> 1)),
            )
            low = r + jnp.where(r >= cut, 16, 0)
            lane_w = jnp.where(north, 111, jnp.where(south, 127, 16 + low))
            lane_e = jnp.where(north, 96, jnp.where(south, 112, low))
            lane = jnp.where(on_w, lane_w, jnp.where(on_e, lane_e, (r & 1) * C + c))
            outside = (north & (lat == 0)) | (south & (lat == n_lat - 1))
            w = jnp.where(outside, 0.0, m[k : k + 1])
            hit = level == lane
            f = jnp.where(hit, w, f)
            q = jnp.where(hit, chunk.astype(F32), q)
        f_ls[:, rows] = f.astype(BF)
        q_ls[:, rows] = q.astype(BF)
        f_sl[pl.ds(g * G, G), :] = f.T.astype(BF)
        q_sl[pl.ds(g * G, G), :] = q.T.astype(BF)
        return carry

    lax.fori_loop(0, groups, spread, 0)
    for k in range(8):
        halo(k).wait_recv()

    def offset(s):
        odd = lax.rem(s, 2)
        step = (s + 1) // 2
        return lax.rem(groups // 2 + step * (1 - 2 * odd) + groups, groups)

    def push(peer, src, dst, send_sem, recv_sem):
        there = pl.ds(me * cap, cap)
        here = pl.ds(peer * cap, cap)

        @pl.when(peer != me)
        def _():
            pltpu.make_async_remote_copy(
                src_ref=src.at[here],
                dst_ref=dst.at[there],
                send_sem=send_sem,
                recv_sem=recv_sem,
                device_id=at(peer),
                device_id_type=MESH,
            ).start()

        @pl.when(peer == me)
        def _():
            pltpu.make_async_copy(src.at[here], dst.at[there], recv_sem).start()

    def interpolate(s, carry):
        g = lax.rem(mine + offset(s), groups)
        rows = pl.ds(g * G, G)
        f, q = f_sl[rows, :], q_sl[rows, :]
        zero = jnp.zeros((G, LANES), BF)
        matrix = jnp.concatenate(
            [jnp.where(q == jnp.array(ch, BF), f, zero) for ch in range(chunks)], axis=1
        )
        column[rows, :] = dot(matrix, cells[...]).astype(BF)
        for i in range(per):
            push(g * per + i, column, pulled, col_send, col_recv.at[mine])
        return carry

    lax.fori_loop(0, groups, interpolate, 0)

    lax.fori_loop(half, parts, components, 0)

    def network(s, carry):
        g = lax.rem(mine - offset(s) + groups, groups)
        rows = pl.ds(g * G, G)
        pltpu.make_async_copy(pulled.at[rows], pulled.at[rows], col_recv.at[g]).wait()
        pre = dot(pulled[rows, :], w_in_ref[...]) + b_in_ref[...]
        sig = jax.nn.sigmoid(pre)
        hidden = (pre * sig).astype(BF)
        sim = dot(hidden, w_out_ref[...]) + b_out_ref[...]
        pcs = dot(onehot[rows, :], pcs_v[...])
        inv = inv_ref[...]
        dep = (sim - pcs) * inv
        dep_slot[rows, :] = dep.astype(BF)
        g_sim = (dep * inv).astype(BF)
        g_hidden = dot(g_sim, w_out_ref[...], ((1,), (1,)))
        g_pre = (g_hidden * sig * (1.0 + pre * (1.0 - sig))).astype(BF)
        g_send[rows, :] = dot(g_pre, w_in_ref[...], ((1,), (1,))).astype(BF)
        for i in range(per):
            push(g * per + i, g_send, g_recv, grad_send, grad_recv.at[mine])
        return carry

    lax.fori_loop(0, groups, network, 0)

    def ordered(i, carry):
        sel = onehot[:, pl.ds(pl.multiple_of(i * G, G), G)]
        dep_v[pl.ds(i * G, G), :] = dot(sel, dep_slot[...], ((0,), (0,))).astype(BF)
        return carry

    lax.fori_loop(0, parts, ordered, 0)
    dep_copy = pltpu.make_async_copy(dep_v, dep_hbm, out_sem.at[0])
    dep_copy.start()

    total[...] = jnp.zeros_like(total)
    block = 7

    def accumulate(s, carry):
        g = lax.rem(mine + offset(s), groups)
        lanes = pl.ds(pl.multiple_of(g * G, G), G)
        rows = pl.ds(g * G, G)
        pltpu.make_async_copy(g_recv.at[rows], g_recv.at[rows], grad_recv.at[g]).wait()
        f, q = f_ls[:, lanes], q_ls[:, lanes]
        zero = jnp.zeros((LANES, G), BF)
        x = g_recv[rows, :]
        for b in range(0, chunks, block):
            last = min(b + block, chunks)
            matrix = jnp.concatenate(
                [jnp.where(q == jnp.array(ch, BF), f, zero) for ch in range(b, last)], axis=0
            )
            total[b * LANES : last * LANES, :] += dot(matrix, x)
        return carry

    lax.fori_loop(0, groups, accumulate, 0)

    starts, at_row = [], 0
    for k in range(8):
        starts.append(at_row)
        at_row += table[k][4]

    def rim(k):
        dl, dc, src, dst, rows = table[k]
        return pltpu.make_async_remote_copy(
            src_ref=total.at[pl.ds(dst, rows)],
            dst_ref=rim_in.at[pl.ds(starts[k], rows)],
            send_sem=rim_send.at[k],
            recv_sem=rim_recv.at[k],
            device_id=near(-dl, -dc),
            device_id_type=MESH,
        )

    for k in range(8):
        rim(k).start()
    for k in range(8):
        rim(k).wait_recv()
    for k in range(8):
        dl, dc, src, dst, rows = table[k]
        if src is not None:
            total[src : src + rows, :] += rim_in[starts[k] : starts[k] + rows, :]
        else:
            first = 0 if dc < 0 else C - 1
            got = rim_in[starts[k] : starts[k] + rows, :]
            got = jnp.concatenate([got[0:cut], got[R : R + 16]], axis=0)
            there = pl.ds(first, R, stride=C)
            total[there, :] = total[there, :] + got
    grad_copy = pltpu.make_async_copy(total.at[pl.ds(0, own)], grad_hbm, out_sem.at[1])
    grad_copy.start()

    for k in range(8):
        halo(k).wait_send()
        rim(k).wait_send()

    def sent(ref, count, sem):
        part = ref.at[pl.ds(0, count)]
        pltpu.make_async_remote_copy(
            src_ref=part, dst_ref=part, send_sem=sem, recv_sem=sem,
            device_id=near(0, 1), device_id_type=MESH,
        ).wait_send()

    sent(send_meta, n - 1, meta_send)
    sent(column, (n - 1) * cap, col_send)
    sent(g_send, (n - 1) * cap, grad_send)
    dep_copy.wait()
    grad_copy.wait()


def per_device(
    n_lat, n_lon,
    spectra, pc_basis, destination, corner_row, corner_col, corner_weight, state, inv_sigma,
    w_in, b_in, w_out, b_out,
):
    n = n_lat * n_lon
    obs, channels = spectra.shape
    R, C, levels = state.shape
    comps = pc_basis.shape[1]
    cap = max(2, 2 * obs // n)
    slots = n * cap
    own = R * C
    ncell = own + 3 * LANES
    assert 2 * C == LANES and R == C and levels == LANES and slots % 256 == 0 and obs % 256 == 0
    meta = jnp.concatenate(
        [
            corner_weight.astype(F32).T,
            corner_row.astype(F32)[None, :],
            corner_col.astype(F32)[None, :],
            destination.astype(F32).T,
            jnp.zeros((1, obs), F32),
        ],
        axis=0,
    )
    vm = pl.BlockSpec(memory_space=pltpu.VMEM)
    hbm = pl.BlockSpec(memory_space=pl.ANY)
    dma = pltpu.SemaphoreType.DMA
    rim_rows = sum(t[4] for t in rim_table(R, C))
    dep, grad = pl.pallas_call(
        functools.partial(kernel, n_lat, n_lon, cap, R, C),
        out_shape=(
            jax.ShapeDtypeStruct((obs, comps), BF),
            jax.ShapeDtypeStruct((own, levels), F32),
        ),
        in_specs=[vm, hbm, hbm, hbm, vm, vm, vm, vm, vm],
        out_specs=(hbm, hbm),
        scratch_shapes=[
            pltpu.VMEM((obs, channels), BF),
            pltpu.VMEM((channels, comps), BF),
            pltpu.VMEM((obs, comps), BF),
            pltpu.VMEM((slots, obs), BF),
            pltpu.VMEM((n, 8, LANES), F32),
            pltpu.VMEM((n, 8, LANES), F32),
            pltpu.VMEM((8, slots), F32),
            pltpu.VMEM((slots, LANES), BF),
            pltpu.VMEM((slots, LANES), BF),
            pltpu.VMEM((LANES, slots), BF),
            pltpu.VMEM((LANES, slots), BF),
            pltpu.VMEM((ncell, levels), BF),
            pltpu.VMEM((2, R + 16, levels), BF),
            pltpu.VMEM((slots, levels), BF),
            pltpu.VMEM((slots, levels), BF),
            pltpu.VMEM((slots, levels), BF),
            pltpu.VMEM((slots, levels), BF),
            pltpu.VMEM((slots, comps), BF),
            pltpu.VMEM((obs, comps), BF),
            pltpu.VMEM((ncell, levels), F32),
            pltpu.VMEM((rim_rows, levels), F32),
            dma((obs // 256 + 1,)),
            dma,
            dma((2,)),
            dma, dma, dma((8,)), dma((8,)),
            dma, dma((slots // 256,)), dma, dma((slots // 256,)),
            dma((8,)), dma((8,)),
        ],
        compiler_params=pltpu.CompilerParams(
            collective_id=0, has_side_effects=True, vmem_limit_bytes=56 * 1024 * 1024
        ),
    )(
        meta, state.reshape(own, levels), spectra, pc_basis,
        w_in, b_in[None, :], w_out, b_out[None, :], inv_sigma[None, :],
    )
    return dep, grad.reshape(R, C, levels)


def solution(mesh):
    n_lat, n_lon = mesh.shape["lat"], mesh.shape["lon"]
    return jax.shard_map(
        functools.partial(per_device, n_lat, n_lon),
        mesh=mesh,
        in_specs=(
            P(("lat", "lon"), None),
            P(),
            P(("lat", "lon"), None),
            P(("lat", "lon")),
            P(("lat", "lon")),
            P(("lat", "lon"), None),
            P("lat", "lon", None),
            P(),
            P(),
            P(),
            P(),
            P(),
        ),
        out_specs=(P(("lat", "lon"), None), P("lat", "lon", None)),
        check_vma=False,
    )
```

```python
import functools

import jax
import jax.numpy as jnp
from jax import lax
from jax.experimental import pallas as pl
from jax.experimental.pallas import tpu as pltpu
from jax.sharding import PartitionSpec as P

MESH = pl.DeviceIdType.MESH
BF = jnp.bfloat16
F32 = jnp.float32
LANES = 128


def dot(a, b, dims=((1,), (0,))):
    return lax.dot_general(a, b, (dims, ((), ())), preferred_element_type=F32)


def rim_table(R, C):
    own = R * C
    ns, west, east = own, own + LANES, own + 2 * LANES
    tall = R + 16
    return [
        (-1, 0, 0, ns, C),
        (1, 0, (R - 1) * C, ns + C, C),
        (0, -1, None, east, tall),
        (0, 1, None, west + 16, tall),
        (-1, -1, 0, east + 112, 16),
        (-1, 1, C - 16, west + 112, 16),
        (1, -1, (R - 1) * C, east + 96, 16),
        (1, 1, own - 16, west + 96, 16),
    ]


def kernel(
    n_lat, n_lon, cap, R, C,
    dest_ref, row_ref, col_ref, weight_ref, state_hbm, spectra_hbm, basis_hbm, w_in_ref, b_in_ref, w_out_ref, b_out_ref, inv_ref,
    dep_ref, grad_ref,
    meta_ref, spectra_v, basis_v, pcs_v, onehot, send_meta, recv_meta, rows_v, f_sl, q_sl, f_ls, q_ls,
    cells, edges, column, pulled, g_send, g_recv, dep_slot, rim_out, rim_in,
    in_sem, state_sem,
    meta_send, meta_recv, halo_send, halo_recv, col_send, col_recv, grad_send, grad_recv,
    rim_send, rim_recv,
):
    n = n_lat * n_lon
    lat = lax.axis_index("lat")
    lon = lax.axis_index("lon")
    me = lat * n_lon + lon
    slots = n * cap
    G = 256
    per = G // cap
    groups = slots // G
    mine = me // per
    own = R * C
    chunks = cells.shape[0] // LANES
    obs = meta_ref.shape[1]
    parts = obs // G
    table = rim_table(R, C)

    def at(peer):
        return (peer // n_lon, lax.rem(peer, n_lon))

    def near(dl, dc):
        return (lax.rem(lat + dl + n_lat, n_lat), lax.rem(lon + dc + n_lon, n_lon))

    barrier = pltpu.get_barrier_semaphore()

    def greet(j, carry):
        peer = lax.rem(me + j, n)
        pl.semaphore_signal(barrier, inc=1, device_id=at(peer), device_id_type=MESH)
        return carry

    lax.fori_loop(1, n, greet, 0)

    state_copy = pltpu.make_async_copy(state_hbm, cells.at[pl.ds(0, own)], state_sem)
    state_copy.start()
    basis_copy = pltpu.make_async_copy(basis_hbm, basis_v, in_sem.at[parts])
    basis_copy.start()

    def spectra_copy(i):
        rows = pl.ds(i * G, G)
        return pltpu.make_async_copy(spectra_hbm.at[rows], spectra_v.at[rows], in_sem.at[i])

    for i in range(parts):
        spectra_copy(i).start()

    dest = dest_ref[...].astype(F32)
    meta_ref[0:4, :] = weight_ref[...].astype(F32)
    meta_ref[4:5, :] = row_ref[...].astype(F32)
    meta_ref[5:6, :] = col_ref[...].astype(F32)
    meta_ref[6:8, :] = jnp.zeros((2, obs), F32)
    before = lax.broadcasted_iota(jnp.int32, (LANES, LANES), 0)
    after = lax.broadcasted_iota(jnp.int32, (LANES, LANES), 1)
    upto = jnp.where(before <= after, 1.0, 0.0).astype(BF)
    tile_id = lax.broadcasted_iota(jnp.int32, (n, LANES), 0).astype(F32)
    carry = jnp.zeros((n, 1), F32)
    places = []
    for b in range(obs // LANES):
        d = dest[:, b * LANES : (b + 1) * LANES]
        oh = jnp.where(tile_id == d, 1.0, 0.0)
        rank = dot(oh.astype(BF), upto) + carry
        slot = jnp.sum(rank * oh, axis=0, keepdims=True) - 1.0
        places.append(d * cap + slot)
        carry = carry + jnp.sum(oh, axis=1, keepdims=True)
    place = jnp.concatenate(places, axis=1)
    meta = meta_ref[...].astype(BF)

    def pack(g, carry):
        ids = (lax.broadcasted_iota(jnp.int32, (G, obs), 0) + g * G).astype(F32)
        sel = jnp.where(ids == place, 1.0, 0.0).astype(BF)
        onehot[pl.ds(g * G, G), :] = sel
        res = dot(meta, sel, ((1,), (1,)))
        for i in range(per):
            piece = res[:, i * cap : (i + 1) * cap]
            send_meta[g * per + i] = jnp.concatenate(
                [piece, jnp.zeros((8, LANES - cap), F32)], axis=1
            )
        return carry

    lax.fori_loop(0, groups, pack, 0)

    pl.semaphore_wait(barrier, n - 1)

    def push_meta(j, carry):
        peer = lax.rem(me + j, n)
        pltpu.make_async_remote_copy(
            src_ref=send_meta.at[peer],
            dst_ref=recv_meta.at[me],
            send_sem=meta_send,
            recv_sem=meta_recv,
            device_id=at(peer),
            device_id_type=MESH,
        ).start()
        return carry

    lax.fori_loop(1, n, push_meta, 0)
    self_meta = pltpu.make_async_copy(send_meta.at[me], recv_meta.at[me], meta_recv)
    self_meta.start()

    west0 = own + LANES
    cells[pl.ds(west0, 16), :] = jnp.zeros((16, LANES), BF)
    cells[pl.ds(west0 + LANES + 80, 16), :] = jnp.zeros((16, LANES), BF)
    state_copy.wait()
    tall = R + 16
    row = lax.broadcasted_iota(jnp.int32, (tall, own), 0)
    cell = lax.broadcasted_iota(jnp.int32, (tall, own), 1)
    cut = R - 16
    row = jnp.where(row < cut, row, jnp.where(row < R, -R, row - 16))
    for s, c in ((0, 0), (1, C - 1)):
        pick = jnp.where(cell == row * C + c, 1.0, 0.0).astype(BF)
        edges[s] = dot(pick, cells[pl.ds(0, own), :]).astype(BF)

    def halo(k):
        dl, dc, src, dst, rows = table[k]
        if src is None:
            source = edges.at[0 if dc < 0 else 1]
        else:
            source = cells.at[pl.ds(src, rows)]
        return pltpu.make_async_remote_copy(
            src_ref=source,
            dst_ref=cells.at[pl.ds(dst, rows)],
            send_sem=halo_send.at[k],
            recv_sem=halo_recv.at[k],
            device_id=near(dl, dc),
            device_id_type=MESH,
        )

    for k in range(8):
        halo(k).start()

    def components(i, carry):
        spectra_copy(i).wait()
        rows = pl.ds(i * G, G)
        pcs_v[rows, :] = dot(spectra_v[rows, :], basis_v[...]).astype(BF)
        return carry

    basis_copy.wait()
    half = 1
    lax.fori_loop(0, half, components, 0)

    pltpu.make_async_copy(recv_meta, recv_meta, meta_recv).wait()
    for s in range(n):
        rows_v[:, s * cap : (s + 1) * cap] = recv_meta[s][:, 0:cap]

    def spread(g, carry):
        rows = pl.ds(pl.multiple_of(g * G, G), G)
        m = rows_v[:, rows]
        r0 = m[4:5].astype(jnp.int32) - 1
        c0 = m[5:6].astype(jnp.int32) - 1
        level = lax.broadcasted_iota(jnp.int32, (LANES, G), 0)
        f = jnp.zeros((LANES, G), F32)
        q = jnp.full((LANES, G), -1.0, F32)
        for k, (dr, dc) in enumerate(((0, 0), (1, 0), (0, 1), (1, 1))):
            r, c = r0 + dr, c0 + dc
            north, south = r < 0, r >= R
            on_w, on_e = c < 0, c >= C
            chunk = jnp.where(
                on_w, chunks - 2,
                jnp.where(on_e, chunks - 1, jnp.where(north | south, chunks - 3, r >> 1)),
            )
            low = r + jnp.where(r >= cut, 16, 0)
            lane_w = jnp.where(north, 111, jnp.where(south, 127, 16 + low))
            lane_e = jnp.where(north, 96, jnp.where(south, 112, low))
            lane = jnp.where(on_w, lane_w, jnp.where(on_e, lane_e, (r & 1) * C + c))
            outside = (north & (lat == 0)) | (south & (lat == n_lat - 1))
            w = jnp.where(outside, 0.0, m[k : k + 1])
            hit = level == lane
            f = jnp.where(hit, w, f)
            q = jnp.where(hit, chunk.astype(F32), q)
        f_ls[:, rows] = f.astype(BF)
        q_ls[:, rows] = q.astype(BF)
        f_sl[pl.ds(g * G, G), :] = f.T.astype(BF)
        q_sl[pl.ds(g * G, G), :] = q.T.astype(BF)
        return carry

    lax.fori_loop(0, groups, spread, 0)
    for k in range(8):
        halo(k).wait_recv()

    def offset(s):
        odd = lax.rem(s, 2)
        step = (s + 1) // 2
        return lax.rem(groups // 2 + step * (1 - 2 * odd) + groups, groups)

    def push(peer, src, dst, send_sem, recv_sem):
        there = pl.ds(me * cap, cap)
        here = pl.ds(peer * cap, cap)

        @pl.when(peer != me)
        def _():
            pltpu.make_async_remote_copy(
                src_ref=src.at[here],
                dst_ref=dst.at[there],
                send_sem=send_sem,
                recv_sem=recv_sem,
                device_id=at(peer),
                device_id_type=MESH,
            ).start()

        @pl.when(peer == me)
        def _():
            pltpu.make_async_copy(src.at[here], dst.at[there], recv_sem).start()

    def interpolate(s, carry):
        g = lax.rem(mine + offset(s), groups)
        rows = pl.ds(g * G, G)
        f, q = f_sl[rows, :], q_sl[rows, :]
        zero = jnp.zeros((G, LANES), BF)
        matrix = jnp.concatenate(
            [jnp.where(q == jnp.array(ch, BF), f, zero) for ch in range(chunks)], axis=1
        )
        column[rows, :] = dot(matrix, cells[...]).astype(BF)
        for i in range(per):
            push(g * per + i, column, pulled, col_send, col_recv.at[mine])
        return carry

    lax.fori_loop(0, groups, interpolate, 0)

    lax.fori_loop(half, parts, components, 0)

    def network(s, carry):
        g = lax.rem(mine - offset(s) + groups, groups)
        rows = pl.ds(g * G, G)
        pltpu.make_async_copy(pulled.at[rows], pulled.at[rows], col_recv.at[g]).wait()
        pre = dot(pulled[rows, :], w_in_ref[...]) + b_in_ref[...]
        sig = jax.nn.sigmoid(pre)
        hidden = (pre * sig).astype(BF)
        sim = dot(hidden, w_out_ref[...]) + b_out_ref[...]
        pcs = dot(onehot[rows, :], pcs_v[...])
        inv = inv_ref[...]
        dep = (sim - pcs) * inv
        dep_slot[rows, :] = dep.astype(BF)
        g_sim = (dep * inv).astype(BF)
        g_hidden = dot(g_sim, w_out_ref[...], ((1,), (1,)))
        g_pre = (g_hidden * sig * (1.0 + pre * (1.0 - sig))).astype(BF)
        g_send[rows, :] = dot(g_pre, w_in_ref[...], ((1,), (1,))).astype(BF)
        for i in range(per):
            push(g * per + i, g_send, g_recv, grad_send, grad_recv.at[mine])
        return carry

    lax.fori_loop(0, groups, network, 0)

    def ordered(i, carry):
        sel = onehot[:, pl.ds(pl.multiple_of(i * G, G), G)]
        dep_ref[pl.ds(i * G, G), :] = dot(sel, dep_slot[...], ((0,), (0,))).astype(BF)
        return carry

    lax.fori_loop(0, parts, ordered, 0)

    grad_ref[...] = jnp.zeros_like(grad_ref)
    rim_out[...] = jnp.zeros_like(rim_out)
    block = 8

    def add_chunks(s, into, first, stop):
        g = lax.rem(mine + offset(s), groups)
        lanes = pl.ds(pl.multiple_of(g * G, G), G)
        f, q = f_ls[:, lanes], q_ls[:, lanes]
        zero = jnp.zeros((LANES, G), BF)
        x = g_recv[pl.ds(g * G, G), :]
        for b in range(first, stop, block):
            last = min(b + block, stop)
            matrix = jnp.concatenate(
                [jnp.where(q == jnp.array(ch, BF), f, zero) for ch in range(b, last)], axis=0
            )
            into[(b - first) * LANES : (last - first) * LANES, :] += dot(matrix, x)

    def accumulate(s, carry):
        g = lax.rem(mine + offset(s), groups)
        rows = pl.ds(g * G, G)
        pltpu.make_async_copy(g_recv.at[rows], g_recv.at[rows], grad_recv.at[g]).wait()
        add_chunks(s, rim_out, chunks - 3, chunks)

        @pl.when(s < groups - 1)
        def _():
            add_chunks(s, grad_ref, 0, chunks - 3)

        return carry

    lax.fori_loop(0, groups, accumulate, 0)

    starts, at_row = [], 0
    for k in range(8):
        starts.append(at_row)
        at_row += table[k][4]

    def rim(k):
        dl, dc, src, dst, rows = table[k]
        return pltpu.make_async_remote_copy(
            src_ref=rim_out.at[pl.ds(dst - own, rows)],
            dst_ref=rim_in.at[pl.ds(starts[k], rows)],
            send_sem=rim_send.at[k],
            recv_sem=rim_recv.at[k],
            device_id=near(-dl, -dc),
            device_id_type=MESH,
        )

    for k in range(8):
        rim(k).start()
    add_chunks(groups - 1, grad_ref, 0, chunks - 3)
    for k in range(8):
        rim(k).wait_recv()
    for k in range(8):
        dl, dc, src, dst, rows = table[k]
        if src is not None:
            grad_ref[src : src + rows, :] += rim_in[starts[k] : starts[k] + rows, :]
        else:
            first = 0 if dc < 0 else C - 1
            got = rim_in[starts[k] : starts[k] + rows, :]
            got = jnp.concatenate([got[0:cut], got[R : R + 16]], axis=0)
            there = pl.ds(first, R, stride=C)
            grad_ref[there, :] = grad_ref[there, :] + got

    for k in range(8):
        halo(k).wait_send()
        rim(k).wait_send()

    def sent(ref, count, sem):
        part = ref.at[pl.ds(0, count)]
        pltpu.make_async_remote_copy(
            src_ref=part, dst_ref=part, send_sem=sem, recv_sem=sem,
            device_id=near(0, 1), device_id_type=MESH,
        ).wait_send()

    sent(send_meta, n - 1, meta_send)
    sent(column, (n - 1) * cap, col_send)
    sent(g_send, (n - 1) * cap, grad_send)


def per_device(
    n_lat, n_lon,
    spectra, pc_basis, destination, corner_row, corner_col, corner_weight, state, inv_sigma,
    w_in, b_in, w_out, b_out,
):
    n = n_lat * n_lon
    obs, channels = spectra.shape
    R, C, levels = state.shape
    comps = pc_basis.shape[1]
    cap = max(2, 2 * obs // n)
    slots = n * cap
    own = R * C
    ncell = own + 3 * LANES
    assert 2 * C == LANES and R == C and levels == LANES and slots % 256 == 0 and obs % 256 == 0
    vm = pl.BlockSpec(memory_space=pltpu.VMEM)
    hbm = pl.BlockSpec(memory_space=pl.ANY)
    dma = pltpu.SemaphoreType.DMA
    rim_rows = sum(t[4] for t in rim_table(R, C))
    dep, grad = pl.pallas_call(
        functools.partial(kernel, n_lat, n_lon, cap, R, C),
        out_shape=(
            jax.ShapeDtypeStruct((obs, comps), BF),
            jax.ShapeDtypeStruct((own, levels), F32),
        ),
        in_specs=[vm, vm, vm, vm, hbm, hbm, hbm, vm, vm, vm, vm, vm],
        out_specs=(vm, vm),
        scratch_shapes=[
            pltpu.VMEM((8, obs), F32),
            pltpu.VMEM((obs, channels), BF),
            pltpu.VMEM((channels, comps), BF),
            pltpu.VMEM((obs, comps), BF),
            pltpu.VMEM((slots, obs), BF),
            pltpu.VMEM((n, 8, LANES), F32),
            pltpu.VMEM((n, 8, LANES), F32),
            pltpu.VMEM((8, slots), F32),
            pltpu.VMEM((slots, LANES), BF),
            pltpu.VMEM((slots, LANES), BF),
            pltpu.VMEM((LANES, slots), BF),
            pltpu.VMEM((LANES, slots), BF),
            pltpu.VMEM((ncell, levels), BF),
            pltpu.VMEM((2, R + 16, levels), BF),
            pltpu.VMEM((slots, levels), BF),
            pltpu.VMEM((slots, levels), BF),
            pltpu.VMEM((slots, levels), BF),
            pltpu.VMEM((slots, levels), BF),
            pltpu.VMEM((slots, comps), BF),
            pltpu.VMEM((3 * LANES, levels), F32),
            pltpu.VMEM((rim_rows, levels), F32),
            dma((obs // 256 + 1,)),
            dma,
            dma, dma, dma((8,)), dma((8,)),
            dma, dma((slots // 256,)), dma, dma((slots // 256,)),
            dma((8,)), dma((8,)),
        ],
        compiler_params=pltpu.CompilerParams(
            collective_id=0, has_side_effects=True, vmem_limit_bytes=46 * 1024 * 1024
        ),
    )(
        destination.T, corner_row[None, :], corner_col[None, :], corner_weight.T,
        state.reshape(own, levels), spectra, pc_basis,
        w_in, b_in[None, :], w_out, b_out[None, :], inv_sigma[None, :],
    )
    return dep, grad.reshape(R, C, levels)


def solution(mesh):
    n_lat, n_lon = mesh.shape["lat"], mesh.shape["lon"]
    return jax.shard_map(
        functools.partial(per_device, n_lat, n_lon),
        mesh=mesh,
        in_specs=(
            P(("lat", "lon"), None),
            P(),
            P(("lat", "lon"), None),
            P(("lat", "lon")),
            P(("lat", "lon")),
            P(("lat", "lon"), None),
            P("lat", "lon", None),
            P(),
            P(),
            P(),
            P(),
            P(),
        ),
        out_specs=(P(("lat", "lon"), None), P("lat", "lon", None)),
        check_vma=False,
    )
```

```python
import functools

import jax
import jax.numpy as jnp
from jax import lax
from jax.experimental import pallas as pl
from jax.experimental.pallas import tpu as pltpu
from jax.sharding import PartitionSpec as P

MESH = pl.DeviceIdType.MESH
BF = jnp.bfloat16
F32 = jnp.float32
LANES = 128


def dot(a, b, dims=((1,), (0,))):
    return lax.dot_general(a, b, (dims, ((), ())), preferred_element_type=F32)


def rim_table(R, C):
    own = R * C
    ns, west, east = own, own + LANES, own + 2 * LANES
    tall = R + 16
    return [
        (-1, 0, 0, ns, C),
        (1, 0, (R - 1) * C, ns + C, C),
        (0, -1, None, east, tall),
        (0, 1, None, west + 16, tall),
        (-1, -1, 0, east + 112, 16),
        (-1, 1, C - 16, west + 112, 16),
        (1, -1, (R - 1) * C, east + 96, 16),
        (1, 1, own - 16, west + 96, 16),
    ]


def kernel(
    n_lat, n_lon, cap, R, C,
    dest_hbm, row_hbm, col_hbm, weight_hbm, w_in_hbm, b_in_hbm, w_out_hbm, b_out_hbm, inv_hbm,
    state_hbm, spectra_hbm, basis_hbm,
    dep_ref, grad_ref,
    dest_ref, row_ref, col_ref, weight_ref, w_in_ref, b_in_ref, w_out_ref, b_out_ref, inv_ref,
    meta_ref, spectra_v, basis_v, pcs_v, onehot, send_meta, recv_meta, rows_v, f_sl, q_sl, f_ls, q_ls,
    cells, edges, column, pulled, g_send, g_recv, dep_slot, rim_out, rim_in,
    small_sem, in_sem, state_sem,
    meta_send, meta_recv, halo_send, halo_recv, col_send, col_recv, grad_send, grad_recv,
    rim_send, rim_recv,
):
    n = n_lat * n_lon
    lat = lax.axis_index("lat")
    lon = lax.axis_index("lon")
    me = lat * n_lon + lon
    slots = n * cap
    G = 256
    per = G // cap
    groups = slots // G
    mine = me // per
    own = R * C
    chunks = cells.shape[0] // LANES
    obs = meta_ref.shape[1]
    parts = obs // G
    table = rim_table(R, C)

    def at(peer):
        return (peer // n_lon, lax.rem(peer, n_lon))

    def near(dl, dc):
        return (lax.rem(lat + dl + n_lat, n_lat), lax.rem(lon + dc + n_lon, n_lon))

    small = [
        pltpu.make_async_copy(src, dst, small_sem.at[i])
        for i, (src, dst) in enumerate(
            (
                (dest_hbm, dest_ref), (row_hbm, row_ref), (col_hbm, col_ref),
                (weight_hbm, weight_ref), (w_in_hbm, w_in_ref), (b_in_hbm, b_in_ref),
                (w_out_hbm, w_out_ref), (b_out_hbm, b_out_ref), (inv_hbm, inv_ref),
            )
        )
    ]
    for copy in small:
        copy.start()
    state_copy = pltpu.make_async_copy(state_hbm, cells.at[pl.ds(0, own)], state_sem)
    state_copy.start()
    basis_copy = pltpu.make_async_copy(basis_hbm, basis_v, in_sem.at[parts])
    basis_copy.start()

    def spectra_copy(i):
        rows = pl.ds(i * G, G)
        return pltpu.make_async_copy(spectra_hbm.at[rows], spectra_v.at[rows], in_sem.at[i])

    for i in range(parts):
        spectra_copy(i).start()

    barrier = pltpu.get_barrier_semaphore()

    def greet(j, carry):
        peer = lax.rem(me + j, n)
        pl.semaphore_signal(barrier, inc=1, device_id=at(peer), device_id_type=MESH)
        return carry

    lax.fori_loop(1, n, greet, 0)

    for copy in small:
        copy.wait()
    dest = dest_ref[...].astype(F32)
    meta_ref[0:4, :] = weight_ref[...].astype(F32)
    meta_ref[4:5, :] = row_ref[...].astype(F32)
    meta_ref[5:6, :] = col_ref[...].astype(F32)
    meta_ref[6:8, :] = jnp.zeros((2, obs), F32)
    before = lax.broadcasted_iota(jnp.int32, (LANES, LANES), 0)
    after = lax.broadcasted_iota(jnp.int32, (LANES, LANES), 1)
    upto = jnp.where(before <= after, 1.0, 0.0).astype(BF)
    tile_id = lax.broadcasted_iota(jnp.int32, (n, LANES), 0).astype(F32)
    carry = jnp.zeros((n, 1), F32)
    places = []
    for b in range(obs // LANES):
        d = dest[:, b * LANES : (b + 1) * LANES]
        oh = jnp.where(tile_id == d, 1.0, 0.0)
        rank = dot(oh.astype(BF), upto) + carry
        slot = jnp.sum(rank * oh, axis=0, keepdims=True) - 1.0
        places.append(d * cap + slot)
        carry = carry + jnp.sum(oh, axis=1, keepdims=True)
    place = jnp.concatenate(places, axis=1)
    meta = meta_ref[...].astype(BF)

    def pack(g, carry):
        ids = (lax.broadcasted_iota(jnp.int32, (G, 1), 0) + g * G).astype(F32)
        sel = jnp.where(ids == place, 1.0, 0.0).astype(BF)
        onehot[pl.ds(g * G, G), :] = sel
        res = dot(meta, sel, ((1,), (1,)))
        for i in range(per):
            piece = res[:, i * cap : (i + 1) * cap]
            send_meta[g * per + i] = jnp.concatenate(
                [piece, jnp.zeros((8, LANES - cap), F32)], axis=1
            )
        return carry

    lax.fori_loop(0, groups, pack, 0)

    pl.semaphore_wait(barrier, n - 1)

    def push_meta(j, carry):
        peer = lax.rem(me + j, n)
        pltpu.make_async_remote_copy(
            src_ref=send_meta.at[peer],
            dst_ref=recv_meta.at[me],
            send_sem=meta_send,
            recv_sem=meta_recv,
            device_id=at(peer),
            device_id_type=MESH,
        ).start()
        return carry

    lax.fori_loop(1, n, push_meta, 0)
    self_meta = pltpu.make_async_copy(send_meta.at[me], recv_meta.at[me], meta_recv)
    self_meta.start()

    west0 = own + LANES
    cells[pl.ds(west0, 16), :] = jnp.zeros((16, LANES), BF)
    cells[pl.ds(west0 + LANES + 80, 16), :] = jnp.zeros((16, LANES), BF)
    state_copy.wait()
    tall = R + 16
    cut = R - 16
    line = lax.broadcasted_iota(jnp.int32, (2 * tall, 1), 0)
    side = jnp.where(line < tall, 0, 1)
    row = line - side * tall
    row = jnp.where(row < cut, row, jnp.where(row < R, -R, row - 16))
    cell = lax.broadcasted_iota(jnp.int32, (2 * tall, own), 1)
    pick = jnp.where(cell == row * C + side * (C - 1), 1.0, 0.0).astype(BF)
    both = dot(pick, cells[pl.ds(0, own), :]).astype(BF)
    edges[0] = both[0:tall]
    edges[1] = both[tall:]

    def halo(k):
        dl, dc, src, dst, rows = table[k]
        if src is None:
            source = edges.at[0 if dc < 0 else 1]
        else:
            source = cells.at[pl.ds(src, rows)]
        return pltpu.make_async_remote_copy(
            src_ref=source,
            dst_ref=cells.at[pl.ds(dst, rows)],
            send_sem=halo_send.at[k],
            recv_sem=halo_recv.at[k],
            device_id=near(dl, dc),
            device_id_type=MESH,
        )

    for k in range(8):
        halo(k).start()

    def components(i, carry):
        spectra_copy(i).wait()
        rows = pl.ds(i * G, G)
        pcs_v[rows, :] = dot(spectra_v[rows, :], basis_v[...]).astype(BF)
        return carry

    basis_copy.wait()
    half = 1
    lax.fori_loop(0, half, components, 0)

    pltpu.make_async_copy(recv_meta, recv_meta, meta_recv).wait()
    for s in range(n):
        rows_v[:, s * cap : (s + 1) * cap] = recv_meta[s][:, 0:cap]

    def spread(g, carry):
        rows = pl.ds(pl.multiple_of(g * G, G), G)
        m = rows_v[:, rows]
        r0 = m[4:5].astype(jnp.int32) - 1
        c0 = m[5:6].astype(jnp.int32) - 1
        level = lax.broadcasted_iota(jnp.int32, (LANES, G), 0)
        f = jnp.zeros((LANES, G), F32)
        q = jnp.full((LANES, G), -1.0, F32)
        for k, (dr, dc) in enumerate(((0, 0), (1, 0), (0, 1), (1, 1))):
            r, c = r0 + dr, c0 + dc
            north, south = r < 0, r >= R
            on_w, on_e = c < 0, c >= C
            chunk = jnp.where(
                on_w, chunks - 2,
                jnp.where(on_e, chunks - 1, jnp.where(north | south, chunks - 3, r >> 1)),
            )
            low = r + jnp.where(r >= cut, 16, 0)
            lane_w = jnp.where(north, 111, jnp.where(south, 127, 16 + low))
            lane_e = jnp.where(north, 96, jnp.where(south, 112, low))
            lane = jnp.where(on_w, lane_w, jnp.where(on_e, lane_e, (r & 1) * C + c))
            outside = (north & (lat == 0)) | (south & (lat == n_lat - 1))
            w = jnp.where(outside, 0.0, m[k : k + 1])
            hit = level == lane
            f = jnp.where(hit, w, f)
            q = jnp.where(hit, chunk.astype(F32), q)
        f_ls[:, rows] = f.astype(BF)
        q_ls[:, rows] = q.astype(BF)
        f_sl[pl.ds(g * G, G), :] = f.T.astype(BF)
        q_sl[pl.ds(g * G, G), :] = q.T.astype(BF)
        return carry

    lax.fori_loop(0, groups, spread, 0)
    for k in range(8):
        halo(k).wait_recv()

    def offset(s):
        odd = lax.rem(s, 2)
        step = (s + 1) // 2
        return lax.rem(groups // 2 + step * (1 - 2 * odd) + groups, groups)

    def push(peer, src, dst, send_sem, recv_sem):
        there = pl.ds(me * cap, cap)
        here = pl.ds(peer * cap, cap)

        @pl.when(peer != me)
        def _():
            pltpu.make_async_remote_copy(
                src_ref=src.at[here],
                dst_ref=dst.at[there],
                send_sem=send_sem,
                recv_sem=recv_sem,
                device_id=at(peer),
                device_id_type=MESH,
            ).start()

        @pl.when(peer == me)
        def _():
            pltpu.make_async_copy(src.at[here], dst.at[there], recv_sem).start()

    def interpolate(s, carry):
        g = lax.rem(mine + offset(s), groups)
        rows = pl.ds(g * G, G)
        f, q = f_sl[rows, :], q_sl[rows, :]
        zero = jnp.zeros((G, LANES), BF)
        matrix = jnp.concatenate(
            [jnp.where(q == jnp.array(ch, BF), f, zero) for ch in range(chunks)], axis=1
        )
        column[rows, :] = dot(matrix, cells[...]).astype(BF)
        for i in range(per):
            push(g * per + i, column, pulled, col_send, col_recv.at[mine])
        return carry

    lax.fori_loop(0, groups, interpolate, 0)

    lax.fori_loop(half, parts, components, 0)

    def group(g):
        rows = pl.ds(g * G, G)
        pre = dot(pulled[rows, :], w_in_ref[...]) + b_in_ref[...]
        sig = 0.5 * jnp.tanh(0.5 * pre) + 0.5
        hid = pre * sig
        sim = dot(hid.astype(BF), w_out_ref[...]) + b_out_ref[...]
        pcs = dot(onehot[rows, :], pcs_v[...])
        inv = inv_ref[...]
        dep = (sim - pcs) * inv
        dep_slot[rows, :] = dep.astype(BF)
        g_sim = (dep * inv).astype(BF)
        g_hidden = dot(g_sim, w_out_ref[...], ((1,), (1,)))
        g_pre = (g_hidden * (sig + hid * (1.0 - sig))).astype(BF)
        g_send[rows, :] = dot(g_pre, w_in_ref[...], ((1,), (1,))).astype(BF)

    together = 2 if groups % 2 == 0 else 1

    def network(s, carry):
        order = [
            lax.rem(mine - offset(s * together + t) + groups, groups) for t in range(together)
        ]
        for g in order:
            rows = pl.ds(g * G, G)
            pltpu.make_async_copy(pulled.at[rows], pulled.at[rows], col_recv.at[g]).wait()
        for g in order:
            group(g)
        for g in order:
            for i in range(per):
                push(g * per + i, g_send, g_recv, grad_send, grad_recv.at[mine])
        return carry

    lax.fori_loop(0, groups // together, network, 0)

    def ordered(i, carry):
        sel = onehot[:, pl.ds(pl.multiple_of(i * G, G), G)]
        dep_ref[pl.ds(i * G, G), :] = dot(sel, dep_slot[...], ((0,), (0,))).astype(BF)
        return carry

    lax.fori_loop(0, parts, ordered, 0)

    grad_ref[...] = jnp.zeros_like(grad_ref)
    rim_out[...] = jnp.zeros_like(rim_out)
    block = 8

    def add_chunks(s, into, first, stop):
        g = lax.rem(mine + offset(s), groups)
        lanes = pl.ds(pl.multiple_of(g * G, G), G)
        f, q = f_ls[:, lanes], q_ls[:, lanes]
        zero = jnp.zeros((LANES, G), BF)
        x = g_recv[pl.ds(g * G, G), :]
        for b in range(first, stop, block):
            last = min(b + block, stop)
            matrix = jnp.concatenate(
                [jnp.where(q == jnp.array(ch, BF), f, zero) for ch in range(b, last)], axis=0
            )
            into[(b - first) * LANES : (last - first) * LANES, :] += dot(matrix, x)

    def accumulate(s, carry):
        g = lax.rem(mine + offset(s), groups)
        rows = pl.ds(g * G, G)
        pltpu.make_async_copy(g_recv.at[rows], g_recv.at[rows], grad_recv.at[g]).wait()
        add_chunks(s, rim_out, chunks - 3, chunks)

        @pl.when(s < groups - 1)
        def _():
            add_chunks(s, grad_ref, 0, chunks - 3)

        return carry

    lax.fori_loop(0, groups, accumulate, 0)

    starts, at_row = [], 0
    for k in range(8):
        starts.append(at_row)
        at_row += table[k][4]

    def rim(k):
        dl, dc, src, dst, rows = table[k]
        return pltpu.make_async_remote_copy(
            src_ref=rim_out.at[pl.ds(dst - own, rows)],
            dst_ref=rim_in.at[pl.ds(starts[k], rows)],
            send_sem=rim_send.at[k],
            recv_sem=rim_recv.at[k],
            device_id=near(-dl, -dc),
            device_id_type=MESH,
        )

    for k in range(8):
        rim(k).start()
    add_chunks(groups - 1, grad_ref, 0, chunks - 3)
    for k in range(8):
        rim(k).wait_recv()
    for k in range(8):
        dl, dc, src, dst, rows = table[k]
        if src is not None:
            grad_ref[src : src + rows, :] += rim_in[starts[k] : starts[k] + rows, :]
        else:
            first = 0 if dc < 0 else C - 1
            got = rim_in[starts[k] : starts[k] + rows, :]
            got = jnp.concatenate([got[0:cut], got[R : R + 16]], axis=0)
            there = pl.ds(first, R, stride=C)
            grad_ref[there, :] = grad_ref[there, :] + got

    for k in range(8):
        halo(k).wait_send()
        rim(k).wait_send()

    def sent(ref, count, sem):
        part = ref.at[pl.ds(0, count)]
        pltpu.make_async_remote_copy(
            src_ref=part, dst_ref=part, send_sem=sem, recv_sem=sem,
            device_id=near(0, 1), device_id_type=MESH,
        ).wait_send()

    sent(send_meta, n - 1, meta_send)
    sent(column, (n - 1) * cap, col_send)
    sent(g_send, (n - 1) * cap, grad_send)


def per_device(
    n_lat, n_lon,
    spectra, pc_basis, destination, corner_row, corner_col, corner_weight, state, inv_sigma,
    w_in, b_in, w_out, b_out,
):
    n = n_lat * n_lon
    obs, channels = spectra.shape
    R, C, levels = state.shape
    comps = pc_basis.shape[1]
    cap = max(2, 2 * obs // n)
    slots = n * cap
    own = R * C
    ncell = own + 3 * LANES
    assert 2 * C == LANES and R == C and levels == LANES and slots % 256 == 0 and obs % 256 == 0
    vm = pl.BlockSpec(memory_space=pltpu.VMEM)
    hbm = pl.BlockSpec(memory_space=pltpu.HBM)
    dma = pltpu.SemaphoreType.DMA
    rim_rows = sum(t[4] for t in rim_table(R, C))
    dep, grad = pl.pallas_call(
        functools.partial(kernel, n_lat, n_lon, cap, R, C),
        out_shape=(
            pltpu.VMEM((obs, comps), BF),
            pltpu.VMEM((own, levels), F32),
        ),
        in_specs=[hbm] * 12,
        out_specs=(vm, vm),
        scratch_shapes=[
            pltpu.VMEM((1, obs), jnp.int32),
            pltpu.VMEM((1, obs), jnp.int32),
            pltpu.VMEM((1, obs), jnp.int32),
            pltpu.VMEM((4, obs), BF),
            pltpu.VMEM(w_in.shape, BF),
            pltpu.VMEM((1, b_in.shape[0]), F32),
            pltpu.VMEM(w_out.shape, BF),
            pltpu.VMEM((1, comps), F32),
            pltpu.VMEM((1, comps), F32),
            pltpu.VMEM((8, obs), F32),
            pltpu.VMEM((obs, channels), BF),
            pltpu.VMEM((channels, comps), BF),
            pltpu.VMEM((obs, comps), BF),
            pltpu.VMEM((slots, obs), BF),
            pltpu.VMEM((n, 8, LANES), F32),
            pltpu.VMEM((n, 8, LANES), F32),
            pltpu.VMEM((8, slots), F32),
            pltpu.VMEM((slots, LANES), BF),
            pltpu.VMEM((slots, LANES), BF),
            pltpu.VMEM((LANES, slots), BF),
            pltpu.VMEM((LANES, slots), BF),
            pltpu.VMEM((ncell, levels), BF),
            pltpu.VMEM((2, R + 16, levels), BF),
            pltpu.VMEM((slots, levels), BF),
            pltpu.VMEM((slots, levels), BF),
            pltpu.VMEM((slots, levels), BF),
            pltpu.VMEM((slots, levels), BF),
            pltpu.VMEM((slots, comps), BF),
            pltpu.VMEM((3 * LANES, levels), F32),
            pltpu.VMEM((rim_rows, levels), F32),
            dma((9,)),
            dma((obs // 256 + 1,)),
            dma,
            dma, dma, dma((8,)), dma((8,)),
            dma, dma((slots // 256,)), dma, dma((slots // 256,)),
            dma((8,)), dma((8,)),
        ],
        compiler_params=pltpu.CompilerParams(
            collective_id=0, has_side_effects=True, vmem_limit_bytes=58 * 1024 * 1024
        ),
    )(
        destination.T, corner_row[None, :], corner_col[None, :], corner_weight.T,
        w_in, b_in[None, :], w_out, b_out[None, :], inv_sigma[None, :],
        state.reshape(own, levels), spectra, pc_basis,
    )
    return dep, grad.reshape(R, C, levels)


def solution(mesh):
    n_lat, n_lon = mesh.shape["lat"], mesh.shape["lon"]
    return jax.shard_map(
        functools.partial(per_device, n_lat, n_lon),
        mesh=mesh,
        in_specs=(
            P(("lat", "lon"), None),
            P(),
            P(("lat", "lon"), None),
            P(("lat", "lon")),
            P(("lat", "lon")),
            P(("lat", "lon"), None),
            P("lat", "lon", None),
            P(),
            P(),
            P(),
            P(),
            P(),
        ),
        out_specs=(P(("lat", "lon"), None), P("lat", "lon", None)),
        check_vma=False,
    )
```

```python
import functools

import jax
import jax.numpy as jnp
from jax import lax
from jax.experimental import pallas as pl
from jax.experimental.pallas import tpu as pltpu
from jax.sharding import PartitionSpec as P

MESH = pl.DeviceIdType.MESH
BF = jnp.bfloat16
F32 = jnp.float32
LANES = 128


def dot(a, b, dims=((1,), (0,))):
    return lax.dot_general(a, b, (dims, ((), ())), preferred_element_type=F32)


def rim_table(R, C):
    own = R * C
    ns, west, east = own, own + LANES, own + 2 * LANES
    tall = R + 16
    return [
        (-1, 0, 0, ns, C),
        (1, 0, (R - 1) * C, ns + C, C),
        (0, -1, None, east, tall),
        (0, 1, None, west + 16, tall),
        (-1, -1, 0, east + 112, 16),
        (-1, 1, C - 16, west + 112, 16),
        (1, -1, (R - 1) * C, east + 96, 16),
        (1, 1, own - 16, west + 96, 16),
    ]


def kernel(
    n_lat, n_lon, cap, R, C,
    dest_hbm, row_hbm, col_hbm, weight_hbm, w_in_hbm, b_in_hbm, w_out_hbm, b_out_hbm, inv_hbm,
    state_hbm, spectra_hbm, basis_hbm,
    dep_ref, grad_ref,
    dest_ref, row_ref, col_ref, weight_ref, w_in_ref, b_in_ref, w_out_ref, b_out_ref, inv_ref,
    meta_ref, spectra_v, basis_v, pcs_v, onehot, send_meta, recv_meta, f_ls, q_ls,
    cells, edges, column, pulled, g_send, g_recv, dep_slot, rim_out, rim_in,
    small_sem, in_sem, state_sem,
    meta_send, meta_recv, halo_send, halo_recv, col_send, col_recv, grad_send, grad_recv,
    rim_send, rim_recv,
):
    n = n_lat * n_lon
    lat = lax.axis_index("lat")
    lon = lax.axis_index("lon")
    me = lat * n_lon + lon
    slots = n * cap
    G = 256
    per = G // cap
    groups = slots // G
    mine = me // per
    own = R * C
    chunks = cells.shape[0] // LANES
    obs = meta_ref.shape[1]
    parts = obs // G
    table = rim_table(R, C)

    def at(peer):
        return (peer // n_lon, lax.rem(peer, n_lon))

    def near(dl, dc):
        return (lax.rem(lat + dl + n_lat, n_lat), lax.rem(lon + dc + n_lon, n_lon))

    small = [
        pltpu.make_async_copy(src, dst, small_sem.at[i])
        for i, (src, dst) in enumerate(
            (
                (dest_hbm, dest_ref), (row_hbm, row_ref), (col_hbm, col_ref),
                (weight_hbm, weight_ref), (w_in_hbm, w_in_ref), (b_in_hbm, b_in_ref),
                (w_out_hbm, w_out_ref), (b_out_hbm, b_out_ref), (inv_hbm, inv_ref),
            )
        )
    ]
    for copy in small:
        copy.start()
    state_copy = pltpu.make_async_copy(state_hbm, cells.at[pl.ds(0, own)], state_sem)
    state_copy.start()
    basis_copy = pltpu.make_async_copy(basis_hbm, basis_v, in_sem.at[parts])
    basis_copy.start()

    def spectra_copy(i):
        rows = pl.ds(i * G, G)
        return pltpu.make_async_copy(spectra_hbm.at[rows], spectra_v.at[rows], in_sem.at[i])

    for i in range(parts):
        spectra_copy(i).start()

    barrier = pltpu.get_barrier_semaphore()

    def greet(j, carry):
        peer = lax.rem(me + j, n)
        pl.semaphore_signal(barrier, inc=1, device_id=at(peer), device_id_type=MESH)
        return carry

    lax.fori_loop(1, n, greet, 0)

    for copy in small:
        copy.wait()
    dest = dest_ref[...].astype(F32)
    weights = weight_ref[...].astype(F32)
    for k, line in enumerate((0, 4, 1, 5)):
        meta_ref[line : line + 1, :] = weights[k : k + 1]
    meta_ref[2:3, :] = row_ref[...].astype(F32)
    meta_ref[6:7, :] = col_ref[...].astype(F32)
    meta_ref[3:4, :] = jnp.zeros((1, obs), F32)
    meta_ref[7:8, :] = jnp.zeros((1, obs), F32)
    before = lax.broadcasted_iota(jnp.int32, (LANES, LANES), 0)
    after = lax.broadcasted_iota(jnp.int32, (LANES, LANES), 1)
    upto = jnp.where(before <= after, 1.0, 0.0).astype(BF)
    tile_id = lax.broadcasted_iota(jnp.int32, (n, LANES), 0).astype(F32)
    carry = jnp.zeros((n, 1), F32)
    places = []
    for b in range(obs // LANES):
        d = dest[:, b * LANES : (b + 1) * LANES]
        oh = jnp.where(tile_id == d, 1.0, 0.0)
        rank = dot(oh.astype(BF), upto) + carry
        slot = jnp.sum(rank * oh, axis=0, keepdims=True) - 1.0
        places.append(d * cap + slot)
        carry = carry + jnp.sum(oh, axis=1, keepdims=True)
    place = jnp.concatenate(places, axis=1)
    meta = meta_ref[...].astype(BF)

    def offset(s):
        odd = lax.rem(s, 2)
        step = (s + 1) // 2
        return lax.rem(groups // 2 + step * (1 - 2 * odd) + groups, groups)

    def push(peer, source, target, send_sem, recv_sem):
        @pl.when(peer != me)
        def _():
            pltpu.make_async_remote_copy(
                src_ref=source,
                dst_ref=target,
                send_sem=send_sem,
                recv_sem=recv_sem,
                device_id=at(peer),
                device_id_type=MESH,
            ).start()

        @pl.when(peer == me)
        def _():
            pltpu.make_async_copy(source, target, recv_sem).start()

    def slots_of(device):
        return pl.ds(device * cap, cap)

    west0 = own + LANES
    cells[pl.ds(west0, 16), :] = jnp.zeros((16, LANES), BF)
    cells[pl.ds(west0 + LANES + 80, 16), :] = jnp.zeros((16, LANES), BF)
    state_copy.wait()
    tall = R + 16
    cut = R - 16
    line = lax.broadcasted_iota(jnp.int32, (2 * tall, 1), 0)
    side = jnp.where(line < tall, 0, 1)
    row = line - side * tall
    row = jnp.where(row < cut, row, jnp.where(row < R, -R, row - 16))
    cell = lax.broadcasted_iota(jnp.int32, (2 * tall, own), 1)
    pick = jnp.where(cell == row * C + side * (C - 1), 1.0, 0.0).astype(BF)
    both = dot(pick, cells[pl.ds(0, own), :]).astype(BF)
    edges[0] = both[0:tall]
    edges[1] = both[tall:]

    def halo(k):
        dl, dc, src, dst, rows = table[k]
        if src is None:
            source = edges.at[0 if dc < 0 else 1]
        else:
            source = cells.at[pl.ds(src, rows)]
        return pltpu.make_async_remote_copy(
            src_ref=source,
            dst_ref=cells.at[pl.ds(dst, rows)],
            send_sem=halo_send.at[k],
            recv_sem=halo_recv.at[k],
            device_id=near(dl, dc),
            device_id_type=MESH,
        )

    pl.semaphore_wait(barrier, n - 1)
    for k in range(8):
        halo(k).start()

    def pack(s, carry):
        g = lax.rem(mine - offset(s) + groups, groups)
        ids = (lax.broadcasted_iota(jnp.int32, (G, 1), 0) + g * G).astype(F32)
        sel = jnp.where(ids == place, 1.0, 0.0).astype(BF)
        onehot[pl.ds(g * G, G), :] = sel
        res = dot(meta, sel, ((1,), (1,)))
        for i in range(per):
            lanes = slice(i * cap, (i + 1) * cap)
            piece = [res[0:4, lanes], res[4:8, lanes]]
            if 2 * cap < LANES:
                piece.append(jnp.zeros((4, LANES - 2 * cap), F32))
            send_meta[g * per + i] = jnp.concatenate(piece, axis=1)
        for i in range(per):
            peer = g * per + i
            push(
                peer, send_meta.at[peer], recv_meta.at[me], meta_send, meta_recv.at[mine]
            )
        return carry

    lax.fori_loop(0, groups, pack, 0)

    for k in range(8):
        halo(k).wait_recv()

    def interpolate(s, carry):
        g = lax.rem(mine + offset(s), groups)
        devices = pl.ds(g * per, per)
        pltpu.make_async_copy(
            recv_meta.at[devices], recv_meta.at[devices], meta_recv.at[g]
        ).wait()
        got = [recv_meta[g * per + i] for i in range(per)]
        top = jnp.concatenate([x[:, 0:cap] for x in got], axis=1)
        low_half = jnp.concatenate([x[:, cap : 2 * cap] for x in got], axis=1)
        r0 = top[2:3].astype(jnp.int32) - 1
        c0 = low_half[2:3].astype(jnp.int32) - 1
        level = lax.broadcasted_iota(jnp.int32, (LANES, G), 0)
        f = jnp.zeros((LANES, G), F32)
        q = jnp.full((LANES, G), -1.0, F32)
        for k, (dr, dc) in enumerate(((0, 0), (1, 0), (0, 1), (1, 1))):
            r, c = r0 + dr, c0 + dc
            north, south = r < 0, r >= R
            on_w, on_e = c < 0, c >= C
            chunk = jnp.where(
                on_w, chunks - 2,
                jnp.where(on_e, chunks - 1, jnp.where(north | south, chunks - 3, r >> 1)),
            )
            low = r + jnp.where(r >= cut, 16, 0)
            lane_w = jnp.where(north, 111, jnp.where(south, 127, 16 + low))
            lane_e = jnp.where(north, 96, jnp.where(south, 112, low))
            lane = jnp.where(on_w, lane_w, jnp.where(on_e, lane_e, (r & 1) * C + c))
            outside = (north & (lat == 0)) | (south & (lat == n_lat - 1))
            weight = (top, low_half)[k % 2][k // 2 : k // 2 + 1]
            w = jnp.where(outside, 0.0, weight)
            hit = level == lane
            f = jnp.where(hit, w, f)
            q = jnp.where(hit, chunk.astype(F32), q)
        lanes = pl.ds(pl.multiple_of(g * G, G), G)
        f_ls[:, lanes] = f.astype(BF)
        q_ls[:, lanes] = q.astype(BF)
        f = f.T.astype(BF)
        q = q.T.astype(BF)
        zero = jnp.zeros((G, LANES), BF)
        matrix = jnp.concatenate(
            [jnp.where(q == jnp.array(ch, BF), f, zero) for ch in range(chunks)], axis=1
        )
        column[pl.ds(g * G, G), :] = dot(matrix, cells[...]).astype(BF)
        for i in range(per):
            peer = g * per + i
            push(
                peer, column.at[slots_of(peer)], pulled.at[slots_of(me)],
                col_send, col_recv.at[mine],
            )
        return carry

    lax.fori_loop(0, groups, interpolate, 0)

    def components(i, carry):
        spectra_copy(i).wait()
        rows = pl.ds(i * G, G)
        pcs_v[rows, :] = dot(spectra_v[rows, :], basis_v[...]).astype(BF)
        return carry

    basis_copy.wait()
    lax.fori_loop(0, parts, components, 0)

    def group(g):
        rows = pl.ds(g * G, G)
        pre = dot(pulled[rows, :], w_in_ref[...]) + b_in_ref[...]
        sig = 0.5 * jnp.tanh(0.5 * pre) + 0.5
        hid = pre * sig
        sim = dot(hid.astype(BF), w_out_ref[...]) + b_out_ref[...]
        pcs = dot(onehot[rows, :], pcs_v[...])
        inv = inv_ref[...]
        dep = (sim - pcs) * inv
        dep_slot[rows, :] = dep.astype(BF)
        g_sim = (dep * inv).astype(BF)
        g_hidden = dot(g_sim, w_out_ref[...], ((1,), (1,)))
        g_pre = (g_hidden * (sig + hid * (1.0 - sig))).astype(BF)
        g_send[rows, :] = dot(g_pre, w_in_ref[...], ((1,), (1,))).astype(BF)

    together = 2 if groups % 2 == 0 else 1

    def network(s, carry):
        order = [
            lax.rem(mine - offset(s * together + t) + groups, groups) for t in range(together)
        ]
        for g in order:
            rows = pl.ds(g * G, G)
            pltpu.make_async_copy(pulled.at[rows], pulled.at[rows], col_recv.at[g]).wait()
        for g in order:
            group(g)
        for g in order:
            for i in range(per):
                peer = g * per + i
                push(
                    peer, g_send.at[slots_of(peer)], g_recv.at[slots_of(me)],
                    grad_send, grad_recv.at[mine],
                )
        return carry

    lax.fori_loop(0, groups // together, network, 0)

    def ordered(i, carry):
        sel = onehot[:, pl.ds(pl.multiple_of(i * G, G), G)]
        dep_ref[pl.ds(i * G, G), :] = dot(sel, dep_slot[...], ((0,), (0,))).astype(BF)
        return carry

    lax.fori_loop(0, parts, ordered, 0)

    grad_ref[...] = jnp.zeros_like(grad_ref)
    rim_out[...] = jnp.zeros_like(rim_out)
    block = 8

    def add_chunks(s, into, first, stop):
        g = lax.rem(mine + offset(s), groups)
        lanes = pl.ds(pl.multiple_of(g * G, G), G)
        f, q = f_ls[:, lanes], q_ls[:, lanes]
        zero = jnp.zeros((LANES, G), BF)
        x = g_recv[pl.ds(g * G, G), :]
        for b in range(first, stop, block):
            last = min(b + block, stop)
            matrix = jnp.concatenate(
                [jnp.where(q == jnp.array(ch, BF), f, zero) for ch in range(b, last)], axis=0
            )
            into[(b - first) * LANES : (last - first) * LANES, :] += dot(matrix, x)

    def accumulate(s, carry):
        g = lax.rem(mine + offset(s), groups)
        rows = pl.ds(g * G, G)
        pltpu.make_async_copy(g_recv.at[rows], g_recv.at[rows], grad_recv.at[g]).wait()
        add_chunks(s, rim_out, chunks - 3, chunks)

        @pl.when(s < groups - 1)
        def _():
            add_chunks(s, grad_ref, 0, chunks - 3)

        return carry

    lax.fori_loop(0, groups, accumulate, 0)

    starts, at_row = [], 0
    for k in range(8):
        starts.append(at_row)
        at_row += table[k][4]

    def rim(k):
        dl, dc, src, dst, rows = table[k]
        return pltpu.make_async_remote_copy(
            src_ref=rim_out.at[pl.ds(dst - own, rows)],
            dst_ref=rim_in.at[pl.ds(starts[k], rows)],
            send_sem=rim_send.at[k],
            recv_sem=rim_recv.at[k],
            device_id=near(-dl, -dc),
            device_id_type=MESH,
        )

    for k in range(8):
        rim(k).start()
    add_chunks(groups - 1, grad_ref, 0, chunks - 3)
    for k in range(8):
        rim(k).wait_recv()
    for k in range(8):
        dl, dc, src, dst, rows = table[k]
        if src is not None:
            grad_ref[src : src + rows, :] += rim_in[starts[k] : starts[k] + rows, :]
        else:
            first = 0 if dc < 0 else C - 1
            got = rim_in[starts[k] : starts[k] + rows, :]
            got = jnp.concatenate([got[0:cut], got[R : R + 16]], axis=0)
            there = pl.ds(first, R, stride=C)
            grad_ref[there, :] = grad_ref[there, :] + got

    for k in range(8):
        halo(k).wait_send()
        rim(k).wait_send()

    def sent(ref, count, sem):
        part = ref.at[pl.ds(0, count)]
        pltpu.make_async_remote_copy(
            src_ref=part, dst_ref=part, send_sem=sem, recv_sem=sem,
            device_id=near(0, 1), device_id_type=MESH,
        ).wait_send()

    sent(send_meta, n - 1, meta_send)
    sent(column, (n - 1) * cap, col_send)
    sent(g_send, (n - 1) * cap, grad_send)


def per_device(
    n_lat, n_lon,
    spectra, pc_basis, destination, corner_row, corner_col, corner_weight, state, inv_sigma,
    w_in, b_in, w_out, b_out,
):
    n = n_lat * n_lon
    obs, channels = spectra.shape
    R, C, levels = state.shape
    comps = pc_basis.shape[1]
    cap = max(2, 2 * obs // n)
    slots = n * cap
    own = R * C
    ncell = own + 3 * LANES
    assert 2 * C == LANES and R == C and levels == LANES and slots % 256 == 0 and obs % 256 == 0
    vm = pl.BlockSpec(memory_space=pltpu.VMEM)
    hbm = pl.BlockSpec(memory_space=pltpu.HBM)
    dma = pltpu.SemaphoreType.DMA
    rim_rows = sum(t[4] for t in rim_table(R, C))
    dep, grad = pl.pallas_call(
        functools.partial(kernel, n_lat, n_lon, cap, R, C),
        out_shape=(
            pltpu.VMEM((obs, comps), BF),
            pltpu.VMEM((own, levels), F32),
        ),
        in_specs=[hbm] * 12,
        out_specs=(vm, vm),
        scratch_shapes=[
            pltpu.VMEM((1, obs), jnp.int32),
            pltpu.VMEM((1, obs), jnp.int32),
            pltpu.VMEM((1, obs), jnp.int32),
            pltpu.VMEM((4, obs), BF),
            pltpu.VMEM(w_in.shape, BF),
            pltpu.VMEM((1, b_in.shape[0]), F32),
            pltpu.VMEM(w_out.shape, BF),
            pltpu.VMEM((1, comps), F32),
            pltpu.VMEM((1, comps), F32),
            pltpu.VMEM((8, obs), F32),
            pltpu.VMEM((obs, channels), BF),
            pltpu.VMEM((channels, comps), BF),
            pltpu.VMEM((obs, comps), BF),
            pltpu.VMEM((slots, obs), BF),
            pltpu.VMEM((n, 4, LANES), F32),
            pltpu.VMEM((n, 4, LANES), F32),
            pltpu.VMEM((LANES, slots), BF),
            pltpu.VMEM((LANES, slots), BF),
            pltpu.VMEM((ncell, levels), BF),
            pltpu.VMEM((2, R + 16, levels), BF),
            pltpu.VMEM((slots, levels), BF),
            pltpu.VMEM((slots, levels), BF),
            pltpu.VMEM((slots, levels), BF),
            pltpu.VMEM((slots, levels), BF),
            pltpu.VMEM((slots, comps), BF),
            pltpu.VMEM((3 * LANES, levels), F32),
            pltpu.VMEM((rim_rows, levels), F32),
            dma((9,)),
            dma((obs // 256 + 1,)),
            dma,
            dma, dma((slots // 256,)), dma((8,)), dma((8,)),
            dma, dma((slots // 256,)), dma, dma((slots // 256,)),
            dma((8,)), dma((8,)),
        ],
        compiler_params=pltpu.CompilerParams(
            collective_id=0, has_side_effects=True, vmem_limit_bytes=58 * 1024 * 1024
        ),
    )(
        destination.T, corner_row[None, :], corner_col[None, :], corner_weight.T,
        w_in, b_in[None, :], w_out, b_out[None, :], inv_sigma[None, :],
        state.reshape(own, levels), spectra, pc_basis,
    )
    return dep, grad.reshape(R, C, levels)


def solution(mesh):
    n_lat, n_lon = mesh.shape["lat"], mesh.shape["lon"]
    return jax.shard_map(
        functools.partial(per_device, n_lat, n_lon),
        mesh=mesh,
        in_specs=(
            P(("lat", "lon"), None),
            P(),
            P(("lat", "lon"), None),
            P(("lat", "lon")),
            P(("lat", "lon")),
            P(("lat", "lon"), None),
            P("lat", "lon", None),
            P(),
            P(),
            P(),
            P(),
            P(),
        ),
        out_specs=(P(("lat", "lon"), None), P("lat", "lon", None)),
        check_vma=False,
    )
```

```python
import functools

import jax
import jax.numpy as jnp
from jax import lax
from jax.experimental import pallas as pl
from jax.experimental.pallas import tpu as pltpu
from jax.sharding import PartitionSpec as P

MESH = pl.DeviceIdType.MESH
BF = jnp.bfloat16
F32 = jnp.float32
LANES = 128


def dot(a, b, dims=((1,), (0,))):
    return lax.dot_general(a, b, (dims, ((), ())), preferred_element_type=F32)


def rim_table(R, C):
    own = R * C
    ns, west, east = own, own + LANES, own + 2 * LANES
    tall = R + 16
    return [
        (-1, 0, 0, ns, C),
        (1, 0, (R - 1) * C, ns + C, C),
        (0, -1, None, east, tall),
        (0, 1, None, west + 16, tall),
        (-1, -1, 0, east + 112, 16),
        (-1, 1, C - 16, west + 112, 16),
        (1, -1, (R - 1) * C, east + 96, 16),
        (1, 1, own - 16, west + 96, 16),
    ]


def kernel(
    n_lat, n_lon, cap, R, C,
    dest_hbm, row_hbm, col_hbm, weight_hbm, w_in_hbm, b_in_hbm, w_out_hbm, b_out_hbm, inv_hbm,
    state_hbm, spectra_hbm, basis_hbm,
    dep_ref, grad_ref,
    dest_ref, row_ref, col_ref, weight_ref, w_in_ref, b_in_ref, w_out_ref, b_out_ref, inv_ref,
    meta_ref, spectra_v, basis_v, pcs_v, onehot, send_meta, recv_meta, f_ls, q_ls,
    cells, wide, edges, in_lower, column, pulled, g_send, g_recv, dep_slot, rim_out, rim_in,
    small_sem, in_sem, state_sem,
    meta_send, meta_recv, halo_send, halo_recv, col_send, col_recv, grad_send, grad_recv,
    rim_send, rim_recv,
):
    n = n_lat * n_lon
    lat = lax.axis_index("lat")
    lon = lax.axis_index("lon")
    me = lat * n_lon + lon
    slots = n * cap
    G = 256
    per = G // cap
    groups = slots // G
    mine = me // per
    own = R * C
    side_chunks = own // 2 // LANES
    chunks = side_chunks + 4
    obs = meta_ref.shape[1]
    parts = obs // G
    table = rim_table(R, C)

    def at(peer):
        return (peer // n_lon, lax.rem(peer, n_lon))

    def near(dl, dc):
        return (lax.rem(lat + dl + n_lat, n_lat), lax.rem(lon + dc + n_lon, n_lon))

    small = [
        pltpu.make_async_copy(src, dst, small_sem.at[i])
        for i, (src, dst) in enumerate(
            (
                (dest_hbm, dest_ref), (row_hbm, row_ref), (col_hbm, col_ref),
                (weight_hbm, weight_ref), (w_in_hbm, w_in_ref), (b_in_hbm, b_in_ref),
                (w_out_hbm, w_out_ref), (b_out_hbm, b_out_ref), (inv_hbm, inv_ref),
            )
        )
    ]
    for copy in small:
        copy.start()
    state_copy = pltpu.make_async_copy(state_hbm, cells.at[pl.ds(0, own)], state_sem)
    state_copy.start()
    basis_copy = pltpu.make_async_copy(basis_hbm, basis_v, in_sem.at[parts])
    basis_copy.start()

    def spectra_copy(i):
        rows = pl.ds(i * G, G)
        return pltpu.make_async_copy(spectra_hbm.at[rows], spectra_v.at[rows], in_sem.at[i])

    for i in range(parts):
        spectra_copy(i).start()

    barrier = pltpu.get_barrier_semaphore()

    def greet(j, carry):
        peer = lax.rem(me + j, n)
        pl.semaphore_signal(barrier, inc=1, device_id=at(peer), device_id_type=MESH)
        return carry

    lax.fori_loop(1, n, greet, 0)

    for copy in small:
        copy.wait()
    dest = dest_ref[...].astype(F32)
    weights = weight_ref[...].astype(F32)
    for k, line in enumerate((0, 4, 1, 5)):
        meta_ref[line : line + 1, :] = weights[k : k + 1]
    meta_ref[2:3, :] = row_ref[...].astype(F32)
    meta_ref[6:7, :] = col_ref[...].astype(F32)
    meta_ref[3:4, :] = jnp.zeros((1, obs), F32)
    meta_ref[7:8, :] = jnp.zeros((1, obs), F32)
    before = lax.broadcasted_iota(jnp.int32, (LANES, LANES), 0)
    after = lax.broadcasted_iota(jnp.int32, (LANES, LANES), 1)
    upto = jnp.where(before <= after, 1.0, 0.0).astype(BF)
    tile_id = lax.broadcasted_iota(jnp.int32, (n, LANES), 0).astype(F32)
    carry = jnp.zeros((n, 1), F32)
    places = []
    for b in range(obs // LANES):
        d = dest[:, b * LANES : (b + 1) * LANES]
        oh = jnp.where(tile_id == d, 1.0, 0.0)
        rank = dot(oh.astype(BF), upto) + carry
        slot = jnp.sum(rank * oh, axis=0, keepdims=True) - 1.0
        places.append(d * cap + slot)
        carry = carry + jnp.sum(oh, axis=1, keepdims=True)
    place = jnp.concatenate(places, axis=1)
    meta = meta_ref[...].astype(BF)

    def offset(s):
        odd = lax.rem(s, 2)
        step = (s + 1) // 2
        return lax.rem(groups // 2 + step * (1 - 2 * odd) + groups, groups)

    def push(peer, source, target, send_sem, recv_sem):
        @pl.when(peer != me)
        def _():
            pltpu.make_async_remote_copy(
                src_ref=source,
                dst_ref=target,
                send_sem=send_sem,
                recv_sem=recv_sem,
                device_id=at(peer),
                device_id_type=MESH,
            ).start()

        @pl.when(peer == me)
        def _():
            pltpu.make_async_copy(source, target, recv_sem).start()

    def slots_of(device):
        return pl.ds(device * cap, cap)

    west0 = own + LANES
    cells[pl.ds(west0, 16), :] = jnp.zeros((16, LANES), BF)
    cells[pl.ds(west0 + LANES + 80, 16), :] = jnp.zeros((16, LANES), BF)
    state_copy.wait()
    tall = R + 16
    cut = R - 16
    line = lax.broadcasted_iota(jnp.int32, (2 * tall, 1), 0)
    side = jnp.where(line < tall, 0, 1)
    row = line - side * tall
    row = jnp.where(row < cut, row, jnp.where(row < R, -R, row - 16))
    cell = lax.broadcasted_iota(jnp.int32, (2 * tall, own), 1)
    pick = jnp.where(cell == row * C + side * (C - 1), 1.0, 0.0).astype(BF)
    both = dot(pick, cells[pl.ds(0, own), :]).astype(BF)
    edges[0] = both[0:tall]
    edges[1] = both[tall:]

    def halo(k):
        dl, dc, src, dst, rows = table[k]
        if src is None:
            source = edges.at[0 if dc < 0 else 1]
        else:
            source = cells.at[pl.ds(src, rows)]
        return pltpu.make_async_remote_copy(
            src_ref=source,
            dst_ref=cells.at[pl.ds(dst, rows)],
            send_sem=halo_send.at[k],
            recv_sem=halo_recv.at[k],
            device_id=near(dl, dc),
            device_id_type=MESH,
        )

    pl.semaphore_wait(barrier, n - 1)
    for k in range(8):
        halo(k).start()

    def pack(s, carry):
        g = lax.rem(mine - offset(s) + groups, groups)
        ids = (lax.broadcasted_iota(jnp.int32, (G, 1), 0) + g * G).astype(F32)
        sel = jnp.where(ids == place, 1.0, 0.0).astype(BF)
        onehot[pl.ds(g * G, G), :] = sel
        res = dot(meta, sel, ((1,), (1,)))
        for i in range(per):
            lanes = slice(i * cap, (i + 1) * cap)
            piece = [res[0:4, lanes], res[4:8, lanes]]
            if 2 * cap < LANES:
                piece.append(jnp.zeros((4, LANES - 2 * cap), F32))
            send_meta[g * per + i] = jnp.concatenate(piece, axis=1)
        for i in range(per):
            peer = g * per + i
            push(
                peer, send_meta.at[peer], recv_meta.at[me], meta_send, meta_recv.at[mine]
            )
        return carry

    lax.fori_loop(0, groups, pack, 0)

    for k in range(8):
        halo(k).wait_recv()
    middle = own // 2
    wide[0:middle, 0:LANES] = cells[0:middle, :]
    wide[0:middle, LANES:] = cells[middle:own, :]
    wide[middle : middle + LANES, 0:LANES] = cells[middle : middle + LANES, :]
    wide[middle : middle + LANES, LANES:] = jnp.zeros((LANES, LANES), BF)
    wide[middle + LANES :, 0:LANES] = cells[own:, :]
    wide[middle + LANES :, LANES:] = cells[own:, :]

    def interpolate(s, carry):
        g = lax.rem(mine + offset(s), groups)
        devices = pl.ds(g * per, per)
        pltpu.make_async_copy(
            recv_meta.at[devices], recv_meta.at[devices], meta_recv.at[g]
        ).wait()
        got = [recv_meta[g * per + i] for i in range(per)]
        top = jnp.concatenate([x[:, 0:cap] for x in got], axis=1)
        low_half = jnp.concatenate([x[:, cap : 2 * cap] for x in got], axis=1)
        r0 = top[2:3].astype(jnp.int32) - 1
        c0 = low_half[2:3].astype(jnp.int32) - 1
        lower = jnp.where(r0 >= R // 2, 1, 0)
        level = lax.broadcasted_iota(jnp.int32, (LANES, G), 0)
        f = jnp.zeros((LANES, G), F32)
        q = jnp.full((LANES, G), -1.0, F32)
        for k, (dr, dc) in enumerate(((0, 0), (1, 0), (0, 1), (1, 1))):
            r, c = r0 + dr, c0 + dc
            north, south = r < 0, r >= R
            on_w, on_e = c < 0, c >= C
            inner = (r >> 1) - lower * side_chunks
            chunk = jnp.where(
                on_w, chunks - 2,
                jnp.where(on_e, chunks - 1, jnp.where(north | south, chunks - 3, inner)),
            )
            low = r + jnp.where(r >= cut, 16, 0)
            lane_w = jnp.where(north, 111, jnp.where(south, 127, 16 + low))
            lane_e = jnp.where(north, 96, jnp.where(south, 112, low))
            lane = jnp.where(on_w, lane_w, jnp.where(on_e, lane_e, (r & 1) * C + c))
            outside = (north & (lat == 0)) | (south & (lat == n_lat - 1))
            weight = (top, low_half)[k % 2][k // 2 : k // 2 + 1]
            w = jnp.where(outside, 0.0, weight)
            hit = level == lane
            f = jnp.where(hit, w, f)
            q = jnp.where(hit, chunk.astype(F32), q)
        lanes = pl.ds(pl.multiple_of(g * G, G), G)
        f_ls[:, lanes] = f.astype(BF)
        q_ls[:, lanes] = q.astype(BF)
        f = f.T.astype(BF)
        q = q.T.astype(BF)
        zero = jnp.zeros((G, LANES), BF)
        matrix = jnp.concatenate(
            [jnp.where(q == jnp.array(ch, BF), f, zero) for ch in range(chunks)], axis=1
        )
        low = jnp.broadcast_to(lower.astype(F32), (LANES, G)).T
        in_lower[pl.ds(g * G, G), :] = low.astype(BF)
        both = dot(matrix, wide[...])
        column[pl.ds(g * G, G), :] = jnp.where(
            low > 0.5, both[:, LANES:], both[:, 0:LANES]
        ).astype(BF)
        for i in range(per):
            peer = g * per + i
            push(
                peer, column.at[slots_of(peer)], pulled.at[slots_of(me)],
                col_send, col_recv.at[mine],
            )
        return carry

    lax.fori_loop(0, groups, interpolate, 0)

    def components(i, carry):
        spectra_copy(i).wait()
        rows = pl.ds(i * G, G)
        pcs_v[rows, :] = dot(spectra_v[rows, :], basis_v[...]).astype(BF)
        return carry

    basis_copy.wait()
    lax.fori_loop(0, parts, components, 0)

    def group(g):
        rows = pl.ds(g * G, G)
        pre = dot(pulled[rows, :], w_in_ref[...]) + b_in_ref[...]
        sig = 0.5 * jnp.tanh(0.5 * pre) + 0.5
        hid = pre * sig
        sim = dot(hid.astype(BF), w_out_ref[...]) + b_out_ref[...]
        pcs = dot(onehot[rows, :], pcs_v[...])
        inv = inv_ref[...]
        dep = (sim - pcs) * inv
        dep_slot[rows, :] = dep.astype(BF)
        g_sim = (dep * inv).astype(BF)
        g_hidden = dot(g_sim, w_out_ref[...], ((1,), (1,)))
        g_pre = (g_hidden * (sig + hid * (1.0 - sig))).astype(BF)
        g_send[rows, :] = dot(g_pre, w_in_ref[...], ((1,), (1,))).astype(BF)

    together = 2 if groups % 2 == 0 else 1

    def network(s, carry):
        order = [
            lax.rem(mine - offset(s * together + t) + groups, groups) for t in range(together)
        ]
        for g in order:
            rows = pl.ds(g * G, G)
            pltpu.make_async_copy(pulled.at[rows], pulled.at[rows], col_recv.at[g]).wait()
        for g in order:
            group(g)
        for g in order:
            for i in range(per):
                peer = g * per + i
                push(
                    peer, g_send.at[slots_of(peer)], g_recv.at[slots_of(me)],
                    grad_send, grad_recv.at[mine],
                )
        return carry

    lax.fori_loop(0, groups // together, network, 0)

    def ordered(i, carry):
        sel = onehot[:, pl.ds(pl.multiple_of(i * G, G), G)]
        dep_ref[pl.ds(i * G, G), :] = dot(sel, dep_slot[...], ((0,), (0,))).astype(BF)
        return carry

    lax.fori_loop(0, parts, ordered, 0)

    grad_ref[...] = jnp.zeros_like(grad_ref)
    rim_out[...] = jnp.zeros_like(rim_out)
    block = 8

    def products(s):
        g = lax.rem(mine + offset(s), groups)
        lanes = pl.ds(pl.multiple_of(g * G, G), G)
        rows = pl.ds(g * G, G)
        f, q = f_ls[:, lanes], q_ls[:, lanes]
        zero = jnp.zeros((LANES, G), BF)
        low, x = in_lower[rows, :], g_recv[rows, :]
        x = jnp.concatenate(
            [jnp.where(low == jnp.array(h, BF), x, jnp.zeros_like(x)) for h in (0, 1)], axis=1
        )

        def part(first, stop):
            matrix = jnp.concatenate(
                [jnp.where(q == jnp.array(ch, BF), f, zero) for ch in range(first, stop)], axis=0
            )
            return dot(matrix, x)

        return part

    def add_rim(s):
        res = products(s)(side_chunks + 1, chunks)
        rim_out[...] += res[:, 0:LANES] + res[:, LANES:]

    def add_tile(s):
        part = products(s)
        for b in range(0, side_chunks, block):
            last = min(b + block, side_chunks)
            res = part(b, last)
            grad_ref[b * LANES : last * LANES, :] += res[:, 0:LANES]
            grad_ref[middle + b * LANES : middle + last * LANES, :] += res[:, LANES:]
        res = part(side_chunks, side_chunks + 1)
        grad_ref[middle : middle + LANES, :] += res[:, 0:LANES]

    def accumulate(s, carry):
        g = lax.rem(mine + offset(s), groups)
        rows = pl.ds(g * G, G)
        pltpu.make_async_copy(g_recv.at[rows], g_recv.at[rows], grad_recv.at[g]).wait()
        add_rim(s)

        @pl.when(s < groups - 1)
        def _():
            add_tile(s)

        return carry

    lax.fori_loop(0, groups, accumulate, 0)

    starts, at_row = [], 0
    for k in range(8):
        starts.append(at_row)
        at_row += table[k][4]

    def rim(k):
        dl, dc, src, dst, rows = table[k]
        return pltpu.make_async_remote_copy(
            src_ref=rim_out.at[pl.ds(dst - own, rows)],
            dst_ref=rim_in.at[pl.ds(starts[k], rows)],
            send_sem=rim_send.at[k],
            recv_sem=rim_recv.at[k],
            device_id=near(-dl, -dc),
            device_id_type=MESH,
        )

    for k in range(8):
        rim(k).start()
    add_tile(groups - 1)
    for k in range(8):
        rim(k).wait_recv()
    for k in range(8):
        dl, dc, src, dst, rows = table[k]
        if src is not None:
            grad_ref[src : src + rows, :] += rim_in[starts[k] : starts[k] + rows, :]
        else:
            first = 0 if dc < 0 else C - 1
            got = rim_in[starts[k] : starts[k] + rows, :]
            got = jnp.concatenate([got[0:cut], got[R : R + 16]], axis=0)
            there = pl.ds(first, R, stride=C)
            grad_ref[there, :] = grad_ref[there, :] + got

    for k in range(8):
        halo(k).wait_send()
        rim(k).wait_send()

    def sent(ref, count, sem):
        part = ref.at[pl.ds(0, count)]
        pltpu.make_async_remote_copy(
            src_ref=part, dst_ref=part, send_sem=sem, recv_sem=sem,
            device_id=near(0, 1), device_id_type=MESH,
        ).wait_send()

    sent(send_meta, n - 1, meta_send)
    sent(column, (n - 1) * cap, col_send)
    sent(g_send, (n - 1) * cap, grad_send)


def per_device(
    n_lat, n_lon,
    spectra, pc_basis, destination, corner_row, corner_col, corner_weight, state, inv_sigma,
    w_in, b_in, w_out, b_out,
):
    n = n_lat * n_lon
    obs, channels = spectra.shape
    R, C, levels = state.shape
    comps = pc_basis.shape[1]
    cap = max(2, 2 * obs // n)
    slots = n * cap
    own = R * C
    ncell = own + 3 * LANES
    assert 2 * C == LANES and R == C and levels == LANES and slots % 256 == 0 and obs % 256 == 0
    vm = pl.BlockSpec(memory_space=pltpu.VMEM)
    hbm = pl.BlockSpec(memory_space=pltpu.HBM)
    dma = pltpu.SemaphoreType.DMA
    rim_rows = sum(t[4] for t in rim_table(R, C))
    dep, grad = pl.pallas_call(
        functools.partial(kernel, n_lat, n_lon, cap, R, C),
        out_shape=(
            pltpu.VMEM((obs, comps), BF),
            pltpu.VMEM((own, levels), F32),
        ),
        in_specs=[hbm] * 12,
        out_specs=(vm, vm),
        scratch_shapes=[
            pltpu.VMEM((1, obs), jnp.int32),
            pltpu.VMEM((1, obs), jnp.int32),
            pltpu.VMEM((1, obs), jnp.int32),
            pltpu.VMEM((4, obs), BF),
            pltpu.VMEM(w_in.shape, BF),
            pltpu.VMEM((1, b_in.shape[0]), F32),
            pltpu.VMEM(w_out.shape, BF),
            pltpu.VMEM((1, comps), F32),
            pltpu.VMEM((1, comps), F32),
            pltpu.VMEM((8, obs), F32),
            pltpu.VMEM((obs, channels), BF),
            pltpu.VMEM((channels, comps), BF),
            pltpu.VMEM((obs, comps), BF),
            pltpu.VMEM((slots, obs), BF),
            pltpu.VMEM((n, 4, LANES), F32),
            pltpu.VMEM((n, 4, LANES), F32),
            pltpu.VMEM((LANES, slots), BF),
            pltpu.VMEM((LANES, slots), BF),
            pltpu.VMEM((ncell, levels), BF),
            pltpu.VMEM((own // 2 + 4 * LANES, 2 * levels), BF),
            pltpu.VMEM((2, R + 16, levels), BF),
            pltpu.VMEM((slots, LANES), BF),
            pltpu.VMEM((slots, levels), BF),
            pltpu.VMEM((slots, levels), BF),
            pltpu.VMEM((slots, levels), BF),
            pltpu.VMEM((slots, levels), BF),
            pltpu.VMEM((slots, comps), BF),
            pltpu.VMEM((3 * LANES, levels), F32),
            pltpu.VMEM((rim_rows, levels), F32),
            dma((9,)),
            dma((obs // 256 + 1,)),
            dma,
            dma, dma((slots // 256,)), dma((8,)), dma((8,)),
            dma, dma((slots // 256,)), dma, dma((slots // 256,)),
            dma((8,)), dma((8,)),
        ],
        compiler_params=pltpu.CompilerParams(
            collective_id=0, has_side_effects=True, vmem_limit_bytes=58 * 1024 * 1024
        ),
    )(
        destination.T, corner_row[None, :], corner_col[None, :], corner_weight.T,
        w_in, b_in[None, :], w_out, b_out[None, :], inv_sigma[None, :],
        state.reshape(own, levels), spectra, pc_basis,
    )
    return dep, grad.reshape(R, C, levels)


def solution(mesh):
    n_lat, n_lon = mesh.shape["lat"], mesh.shape["lon"]
    return jax.shard_map(
        functools.partial(per_device, n_lat, n_lon),
        mesh=mesh,
        in_specs=(
            P(("lat", "lon"), None),
            P(),
            P(("lat", "lon"), None),
            P(("lat", "lon")),
            P(("lat", "lon")),
            P(("lat", "lon"), None),
            P("lat", "lon", None),
            P(),
            P(),
            P(),
            P(),
            P(),
        ),
        out_specs=(P(("lat", "lon"), None), P("lat", "lon", None)),
        check_vma=False,
    )
```

```python
import functools

import jax
import jax.numpy as jnp
from jax import lax
from jax.experimental import pallas as pl
from jax.experimental.pallas import tpu as pltpu
from jax.sharding import PartitionSpec as P

MESH = pl.DeviceIdType.MESH
BF = jnp.bfloat16
F32 = jnp.float32
LANES = 128


def dot(a, b, dims=((1,), (0,))):
    return lax.dot_general(a, b, (dims, ((), ())), preferred_element_type=F32)


def rim_table(R, C):
    own = R * C
    ns, west, east = own, own + LANES, own + 2 * LANES
    tall = R + 16
    return [
        (-1, 0, 0, ns, C),
        (1, 0, (R - 1) * C, ns + C, C),
        (0, -1, None, east, tall),
        (0, 1, None, west + 16, tall),
        (-1, -1, 0, east + 112, 16),
        (-1, 1, C - 16, west + 112, 16),
        (1, -1, (R - 1) * C, east + 96, 16),
        (1, 1, own - 16, west + 96, 16),
    ]


def kernel(
    n_lat, n_lon, cap, R, C,
    dest_hbm, row_hbm, col_hbm, weight_hbm, w_in_hbm, b_in_hbm, w_out_hbm, b_out_hbm, inv_hbm,
    state_hbm, spectra_hbm, basis_hbm,
    dep_ref, grad_ref,
    dest_ref, row_ref, col_ref, weight_ref, w_in_ref, b_in_ref, w_out_ref, b_out_ref, inv_ref,
    meta_ref, spectra_v, basis_v, pcs_v, onehot, send_meta, recv_meta, f_ls, q_ls,
    cells, wide, edges, in_lower, column, pulled, g_send, g_recv, dep_slot, rim_out, rim_in,
    small_sem, in_sem, state_sem,
    meta_send, meta_recv, halo_send, halo_recv, col_send, col_recv, grad_send, grad_recv,
    rim_send, rim_recv,
):
    n = n_lat * n_lon
    lat = lax.axis_index("lat")
    lon = lax.axis_index("lon")
    me = lat * n_lon + lon
    slots = n * cap
    G = 256
    per = G // cap
    groups = slots // G
    mine = me // per
    own = R * C
    side_chunks = own // 2 // LANES
    chunks = side_chunks + 4
    obs = meta_ref.shape[1]
    parts = obs // G
    table = rim_table(R, C)

    def at(peer):
        return (peer // n_lon, lax.rem(peer, n_lon))

    def near(dl, dc):
        return (lax.rem(lat + dl + n_lat, n_lat), lax.rem(lon + dc + n_lon, n_lon))

    small = [
        pltpu.make_async_copy(src, dst, small_sem.at[i])
        for i, (src, dst) in enumerate(
            (
                (dest_hbm, dest_ref), (row_hbm, row_ref), (col_hbm, col_ref),
                (weight_hbm, weight_ref), (w_in_hbm, w_in_ref), (b_in_hbm, b_in_ref),
                (w_out_hbm, w_out_ref), (b_out_hbm, b_out_ref), (inv_hbm, inv_ref),
            )
        )
    ]
    for copy in small:
        copy.start()
    state_copy = pltpu.make_async_copy(state_hbm, cells.at[pl.ds(0, own)], state_sem)
    state_copy.start()
    basis_copy = pltpu.make_async_copy(basis_hbm, basis_v, in_sem.at[parts])
    basis_copy.start()

    def spectra_copy(i):
        rows = pl.ds(i * G, G)
        return pltpu.make_async_copy(spectra_hbm.at[rows], spectra_v.at[rows], in_sem.at[i])

    for i in range(parts):
        spectra_copy(i).start()

    barrier = pltpu.get_barrier_semaphore()

    def greet(j, carry):
        peer = lax.rem(me + j, n)
        pl.semaphore_signal(barrier, inc=1, device_id=at(peer), device_id_type=MESH)
        return carry

    lax.fori_loop(1, n, greet, 0)

    for copy in small:
        copy.wait()
    dest = dest_ref[...].astype(F32)
    weights = weight_ref[...].astype(F32)
    for k, line in enumerate((0, 4, 1, 5)):
        meta_ref[line : line + 1, :] = weights[k : k + 1]
    meta_ref[2:3, :] = row_ref[...].astype(F32)
    meta_ref[6:7, :] = col_ref[...].astype(F32)
    meta_ref[3:4, :] = jnp.zeros((1, obs), F32)
    meta_ref[7:8, :] = jnp.zeros((1, obs), F32)
    before = lax.broadcasted_iota(jnp.int32, (LANES, LANES), 0)
    after = lax.broadcasted_iota(jnp.int32, (LANES, LANES), 1)
    upto = jnp.where(before <= after, 1.0, 0.0).astype(BF)
    tile_id = lax.broadcasted_iota(jnp.int32, (n, LANES), 0).astype(F32)
    carry = jnp.zeros((n, 1), F32)
    places = []
    for b in range(obs // LANES):
        d = dest[:, b * LANES : (b + 1) * LANES]
        oh = jnp.where(tile_id == d, 1.0, 0.0)
        rank = dot(oh.astype(BF), upto) + carry
        slot = jnp.sum(rank * oh, axis=0, keepdims=True) - 1.0
        places.append(d * cap + slot)
        carry = carry + jnp.sum(oh, axis=1, keepdims=True)
    place = jnp.concatenate(places, axis=1)
    meta = meta_ref[...].astype(BF)

    def offset(s):
        odd = lax.rem(s, 2)
        step = (s + 1) // 2
        return lax.rem(groups // 2 + step * (1 - 2 * odd) + groups, groups)

    def push(peer, source, target, send_sem, recv_sem):
        @pl.when(peer != me)
        def _():
            pltpu.make_async_remote_copy(
                src_ref=source,
                dst_ref=target,
                send_sem=send_sem,
                recv_sem=recv_sem,
                device_id=at(peer),
                device_id_type=MESH,
            ).start()

        @pl.when(peer == me)
        def _():
            pltpu.make_async_copy(source, target, recv_sem).start()

    def slots_of(device):
        return pl.ds(device * cap, cap)

    west0 = own + LANES
    cells[pl.ds(west0, 16), :] = jnp.zeros((16, LANES), BF)
    cells[pl.ds(west0 + LANES + 80, 16), :] = jnp.zeros((16, LANES), BF)
    state_copy.wait()
    tall = R + 16
    cut = R - 16
    line = lax.broadcasted_iota(jnp.int32, (2 * tall, 1), 0)
    side = jnp.where(line < tall, 0, 1)
    row = line - side * tall
    row = jnp.where(row < cut, row, jnp.where(row < R, -R, row - 16))
    cell = lax.broadcasted_iota(jnp.int32, (2 * tall, own), 1)
    pick = jnp.where(cell == row * C + side * (C - 1), 1.0, 0.0).astype(BF)
    both = dot(pick, cells[pl.ds(0, own), :]).astype(BF)
    edges[0] = both[0:tall]
    edges[1] = both[tall:]

    def halo(k):
        dl, dc, src, dst, rows = table[k]
        if src is None:
            source = edges.at[0 if dc < 0 else 1]
        else:
            source = cells.at[pl.ds(src, rows)]
        return pltpu.make_async_remote_copy(
            src_ref=source,
            dst_ref=cells.at[pl.ds(dst, rows)],
            send_sem=halo_send.at[k],
            recv_sem=halo_recv.at[k],
            device_id=near(dl, dc),
            device_id_type=MESH,
        )

    grad_ref[...] = jnp.zeros_like(grad_ref)
    rim_out[...] = jnp.zeros_like(rim_out)
    pl.semaphore_wait(barrier, n - 1)
    for k in range(8):
        halo(k).start()

    def pack(s, carry):
        g = lax.rem(mine - offset(s) + groups, groups)
        ids = (lax.broadcasted_iota(jnp.int32, (G, 1), 0) + g * G).astype(F32)
        sel = jnp.where(ids == place, 1.0, 0.0).astype(BF)
        onehot[pl.ds(g * G, G), :] = sel
        res = dot(meta, sel, ((1,), (1,)))
        for i in range(per):
            lanes = slice(i * cap, (i + 1) * cap)
            piece = [res[0:4, lanes], res[4:8, lanes]]
            if 2 * cap < LANES:
                piece.append(jnp.zeros((4, LANES - 2 * cap), F32))
            send_meta[g * per + i] = jnp.concatenate(piece, axis=1)
        for i in range(per):
            peer = g * per + i
            push(
                peer, send_meta.at[peer], recv_meta.at[me], meta_send, meta_recv.at[mine]
            )
        return carry

    lax.fori_loop(0, groups, pack, 0)

    for k in range(8):
        halo(k).wait_recv()
    middle = own // 2
    wide[0:middle, 0:LANES] = cells[0:middle, :]
    wide[0:middle, LANES:] = cells[middle:own, :]
    wide[middle : middle + LANES, 0:LANES] = cells[middle : middle + LANES, :]
    wide[middle : middle + LANES, LANES:] = jnp.zeros((LANES, LANES), BF)
    wide[middle + LANES :, 0:LANES] = cells[own:, :]
    wide[middle + LANES :, LANES:] = cells[own:, :]

    def interpolate(s, carry):
        g = lax.rem(mine + offset(s), groups)
        devices = pl.ds(g * per, per)
        pltpu.make_async_copy(
            recv_meta.at[devices], recv_meta.at[devices], meta_recv.at[g]
        ).wait()
        got = [recv_meta[g * per + i] for i in range(per)]
        top = jnp.concatenate([x[:, 0:cap] for x in got], axis=1)
        low_half = jnp.concatenate([x[:, cap : 2 * cap] for x in got], axis=1)
        r0 = top[2:3].astype(jnp.int32) - 1
        c0 = low_half[2:3].astype(jnp.int32) - 1
        lower = jnp.where(r0 >= R // 2, 1, 0)
        level = lax.broadcasted_iota(jnp.int32, (LANES, G), 0)
        f = jnp.zeros((LANES, G), F32)
        q = jnp.full((LANES, G), -1.0, F32)
        for k, (dr, dc) in enumerate(((0, 0), (1, 0), (0, 1), (1, 1))):
            r, c = r0 + dr, c0 + dc
            north, south = r < 0, r >= R
            on_w, on_e = c < 0, c >= C
            inner = (r >> 1) - lower * side_chunks
            chunk = jnp.where(
                on_w, chunks - 2,
                jnp.where(on_e, chunks - 1, jnp.where(north | south, chunks - 3, inner)),
            )
            low = r + jnp.where(r >= cut, 16, 0)
            lane_w = jnp.where(north, 111, jnp.where(south, 127, 16 + low))
            lane_e = jnp.where(north, 96, jnp.where(south, 112, low))
            lane = jnp.where(on_w, lane_w, jnp.where(on_e, lane_e, (r & 1) * C + c))
            outside = (north & (lat == 0)) | (south & (lat == n_lat - 1))
            weight = (top, low_half)[k % 2][k // 2 : k // 2 + 1]
            w = jnp.where(outside, 0.0, weight)
            hit = level == lane
            f = jnp.where(hit, w, f)
            q = jnp.where(hit, chunk.astype(F32), q)
        lanes = pl.ds(pl.multiple_of(g * G, G), G)
        f_ls[:, lanes] = f.astype(BF)
        q_ls[:, lanes] = q.astype(BF)
        f = f.T.astype(BF)
        q = q.T.astype(BF)
        zero = jnp.zeros((G, LANES), BF)
        matrix = jnp.concatenate(
            [jnp.where(q == jnp.array(ch, BF), f, zero) for ch in range(chunks)], axis=1
        )
        low = jnp.broadcast_to(lower.astype(F32), (LANES, G)).T
        in_lower[pl.ds(g * G, G), :] = low.astype(BF)
        both = dot(matrix, wide[...])
        column[pl.ds(g * G, G), :] = jnp.where(
            low > 0.5, both[:, LANES:], both[:, 0:LANES]
        ).astype(BF)
        for i in range(per):
            peer = g * per + i
            push(
                peer, column.at[slots_of(peer)], pulled.at[slots_of(me)],
                col_send, col_recv.at[mine],
            )
        return carry

    lax.fori_loop(0, groups, interpolate, 0)

    def components(i, carry):
        spectra_copy(i).wait()
        rows = pl.ds(i * G, G)
        pcs_v[rows, :] = dot(spectra_v[rows, :], basis_v[...]).astype(BF)
        return carry

    basis_copy.wait()
    lax.fori_loop(0, parts, components, 0)

    def group(g):
        rows = pl.ds(g * G, G)
        pre = dot(pulled[rows, :], w_in_ref[...]) + b_in_ref[...]
        sig = 0.5 * jnp.tanh(0.5 * pre) + 0.5
        hid = pre * sig
        sim = dot(hid.astype(BF), w_out_ref[...]) + b_out_ref[...]
        pcs = dot(onehot[rows, :], pcs_v[...])
        inv = inv_ref[...]
        dep = (sim - pcs) * inv
        dep_slot[rows, :] = dep.astype(BF)
        g_sim = (dep * inv).astype(BF)
        g_hidden = dot(g_sim, w_out_ref[...], ((1,), (1,)))
        g_pre = (g_hidden * (sig + hid * (1.0 - sig))).astype(BF)
        g_send[rows, :] = dot(g_pre, w_in_ref[...], ((1,), (1,))).astype(BF)

    together = 2 if groups % 2 == 0 else 1

    def network(s, carry):
        order = [
            lax.rem(mine - offset(s * together + t) + groups, groups) for t in range(together)
        ]
        for g in order:
            rows = pl.ds(g * G, G)
            pltpu.make_async_copy(pulled.at[rows], pulled.at[rows], col_recv.at[g]).wait()
        for g in order:
            group(g)
        for g in order:
            for i in range(per):
                peer = g * per + i
                push(
                    peer, g_send.at[slots_of(peer)], g_recv.at[slots_of(me)],
                    grad_send, grad_recv.at[mine],
                )
        return carry

    lax.fori_loop(0, groups // together, network, 0)

    def ordered(i, carry):
        sel = onehot[:, pl.ds(pl.multiple_of(i * G, G), G)]
        dep_ref[pl.ds(i * G, G), :] = dot(sel, dep_slot[...], ((0,), (0,))).astype(BF)
        return carry

    early = parts // 2
    lax.fori_loop(0, early, ordered, 0)

    block = 8

    def products(s):
        g = lax.rem(mine + offset(s), groups)
        lanes = pl.ds(pl.multiple_of(g * G, G), G)
        rows = pl.ds(g * G, G)
        f, q = f_ls[:, lanes], q_ls[:, lanes]
        zero = jnp.zeros((LANES, G), BF)
        low, x = in_lower[rows, :], g_recv[rows, :]
        x = jnp.concatenate(
            [jnp.where(low == jnp.array(h, BF), x, jnp.zeros_like(x)) for h in (0, 1)], axis=1
        )

        def part(first, stop):
            matrix = jnp.concatenate(
                [jnp.where(q == jnp.array(ch, BF), f, zero) for ch in range(first, stop)], axis=0
            )
            return dot(matrix, x)

        return part

    def add_rim(s):
        res = products(s)(side_chunks + 1, chunks)
        rim_out[...] += res[:, 0:LANES] + res[:, LANES:]

    def add_tile(s):
        part = products(s)
        for b in range(0, side_chunks, block):
            last = min(b + block, side_chunks)
            res = part(b, last)
            grad_ref[b * LANES : last * LANES, :] += res[:, 0:LANES]
            grad_ref[middle + b * LANES : middle + last * LANES, :] += res[:, LANES:]
        res = part(side_chunks, side_chunks + 1)
        grad_ref[middle : middle + LANES, :] += res[:, 0:LANES]

    def accumulate(s, carry):
        g = lax.rem(mine + offset(s), groups)
        rows = pl.ds(g * G, G)
        pltpu.make_async_copy(g_recv.at[rows], g_recv.at[rows], grad_recv.at[g]).wait()
        add_rim(s)

        @pl.when(s < groups - 1)
        def _():
            add_tile(s)

        return carry

    lax.fori_loop(0, groups, accumulate, 0)

    starts, at_row = [], 0
    for k in range(8):
        starts.append(at_row)
        at_row += table[k][4]

    def rim(k):
        dl, dc, src, dst, rows = table[k]
        return pltpu.make_async_remote_copy(
            src_ref=rim_out.at[pl.ds(dst - own, rows)],
            dst_ref=rim_in.at[pl.ds(starts[k], rows)],
            send_sem=rim_send.at[k],
            recv_sem=rim_recv.at[k],
            device_id=near(-dl, -dc),
            device_id_type=MESH,
        )

    for k in range(8):
        rim(k).start()
    add_tile(groups - 1)
    lax.fori_loop(early, parts, ordered, 0)
    for k in range(8):
        rim(k).wait_recv()
    for k in range(8):
        dl, dc, src, dst, rows = table[k]
        if src is not None:
            grad_ref[src : src + rows, :] += rim_in[starts[k] : starts[k] + rows, :]
        else:
            first = 0 if dc < 0 else C - 1
            got = rim_in[starts[k] : starts[k] + rows, :]
            got = jnp.concatenate([got[0:cut], got[R : R + 16]], axis=0)
            there = pl.ds(first, R, stride=C)
            grad_ref[there, :] = grad_ref[there, :] + got

    for k in range(8):
        halo(k).wait_send()
        rim(k).wait_send()

    def sent(ref, count, sem):
        part = ref.at[pl.ds(0, count)]
        pltpu.make_async_remote_copy(
            src_ref=part, dst_ref=part, send_sem=sem, recv_sem=sem,
            device_id=near(0, 1), device_id_type=MESH,
        ).wait_send()

    sent(send_meta, n - 1, meta_send)
    sent(column, (n - 1) * cap, col_send)
    sent(g_send, (n - 1) * cap, grad_send)


def per_device(
    n_lat, n_lon,
    spectra, pc_basis, destination, corner_row, corner_col, corner_weight, state, inv_sigma,
    w_in, b_in, w_out, b_out,
):
    n = n_lat * n_lon
    obs, channels = spectra.shape
    R, C, levels = state.shape
    comps = pc_basis.shape[1]
    cap = max(2, 2 * obs // n)
    slots = n * cap
    own = R * C
    ncell = own + 3 * LANES
    assert 2 * C == LANES and R == C and levels == LANES and slots % 256 == 0 and obs % 256 == 0
    vm = pl.BlockSpec(memory_space=pltpu.VMEM)
    hbm = pl.BlockSpec(memory_space=pltpu.HBM)
    dma = pltpu.SemaphoreType.DMA
    rim_rows = sum(t[4] for t in rim_table(R, C))
    dep, grad = pl.pallas_call(
        functools.partial(kernel, n_lat, n_lon, cap, R, C),
        out_shape=(
            pltpu.VMEM((obs, comps), BF),
            pltpu.VMEM((own, levels), F32),
        ),
        in_specs=[hbm] * 12,
        out_specs=(vm, vm),
        scratch_shapes=[
            pltpu.VMEM((1, obs), jnp.int32),
            pltpu.VMEM((1, obs), jnp.int32),
            pltpu.VMEM((1, obs), jnp.int32),
            pltpu.VMEM((4, obs), BF),
            pltpu.VMEM(w_in.shape, BF),
            pltpu.VMEM((1, b_in.shape[0]), F32),
            pltpu.VMEM(w_out.shape, BF),
            pltpu.VMEM((1, comps), F32),
            pltpu.VMEM((1, comps), F32),
            pltpu.VMEM((8, obs), F32),
            pltpu.VMEM((obs, channels), BF),
            pltpu.VMEM((channels, comps), BF),
            pltpu.VMEM((obs, comps), BF),
            pltpu.VMEM((slots, obs), BF),
            pltpu.VMEM((n, 4, LANES), F32),
            pltpu.VMEM((n, 4, LANES), F32),
            pltpu.VMEM((LANES, slots), BF),
            pltpu.VMEM((LANES, slots), BF),
            pltpu.VMEM((ncell, levels), BF),
            pltpu.VMEM((own // 2 + 4 * LANES, 2 * levels), BF),
            pltpu.VMEM((2, R + 16, levels), BF),
            pltpu.VMEM((slots, LANES), BF),
            pltpu.VMEM((slots, levels), BF),
            pltpu.VMEM((slots, levels), BF),
            pltpu.VMEM((slots, levels), BF),
            pltpu.VMEM((slots, levels), BF),
            pltpu.VMEM((slots, comps), BF),
            pltpu.VMEM((3 * LANES, levels), F32),
            pltpu.VMEM((rim_rows, levels), F32),
            dma((9,)),
            dma((obs // 256 + 1,)),
            dma,
            dma, dma((slots // 256,)), dma((8,)), dma((8,)),
            dma, dma((slots // 256,)), dma, dma((slots // 256,)),
            dma((8,)), dma((8,)),
        ],
        compiler_params=pltpu.CompilerParams(
            collective_id=0, has_side_effects=True, vmem_limit_bytes=58 * 1024 * 1024
        ),
    )(
        destination.T, corner_row[None, :], corner_col[None, :], corner_weight.T,
        w_in, b_in[None, :], w_out, b_out[None, :], inv_sigma[None, :],
        state.reshape(own, levels), spectra, pc_basis,
    )
    return dep, grad.reshape(R, C, levels)


def solution(mesh):
    n_lat, n_lon = mesh.shape["lat"], mesh.shape["lon"]
    return jax.shard_map(
        functools.partial(per_device, n_lat, n_lon),
        mesh=mesh,
        in_specs=(
            P(("lat", "lon"), None),
            P(),
            P(("lat", "lon"), None),
            P(("lat", "lon")),
            P(("lat", "lon")),
            P(("lat", "lon"), None),
            P("lat", "lon", None),
            P(),
            P(),
            P(),
            P(),
            P(),
        ),
        out_specs=(P(("lat", "lon"), None), P("lat", "lon", None)),
        check_vma=False,
    )
```
